32 devices in a mesh: grp: 4 (over y, core), dev: 8 (over z, x).
Axes of the slice: x: 2, y: 2, z: 4, core: 2. Of those that a mesh axis runs over, the one named last changes fastest.
Arguments:
- tiles: bfloat16 [16384, 128, 128], P(('grp', 'dev')), may hold values from -0.125 to 0.125
- tile_ray: int32 [16384], P(('grp', 'dev')), may hold values from 0 to 31, as said below
- tile_col: int32 [16384], P(('grp', 'dev')), may hold values from 0 to 23, as said below
- touched: int32 [768], P(('grp', 'dev')), may hold values from 0 to 2047, as said below
- home: int32 [2048], replicated, may hold values from 0 to 2047, as said below
- sketch: bfloat16 [262144, 128], P(('grp', 'dev')), may hold values from -6 to 6
Outputs:
- basis: float32 [262144, 128], P(('grp', 'dev'))
- r_factor: float32 [128, 128], replicated
The draws below stay inside these ranges and needn't reach their ends.
Inputs may be any that keep to these rules, and one draw needn't show every extreme that they name: `home`: A permutation that maps each region of 512 consecutive voxel blocks, g * 512 to (g + 1) * 512 - 1, onto the same range of positions. The 24 entries of device i along grp+dev are distinct voxel blocks whose positions home[v] lie in the region of its group g = i // 8; at most 3 of them have positions stored on any one device (position // 64), and in every group one device stores 3 of the touched blocks of every device of the group. On each device the pairs (tile_ray, tile_col) are distinct. `tile_col`: indexes the device's own 24 entries of touched.
All inputs are finite; a program needn't handle non-finite values.
Results may differ from the reference program's by a relative error of at most 0.0017.
Values may be sent and summed in bfloat16 or wider, within the bound.
No kernel may reach another device: no remote copies, remote signals or barrier semaphores. Data moves between devices by JAX's collectives and lax.ppermute only.
A program may use at most 192 MiB of HBM per device.

```python
import math
import jax
import jax.numpy as jnp
from jax import lax

BLK = 128
K = 128
VBLK_DEV = 64
NTOUCH = 24
CAP = 3
TILES_RB = 16
RB_DEV = 32
NT_DEV = 512
REGION = 512
VBLOCKS = 2048
VOX = 262144
RAYBLK = 1024
TILES = 16384
DEVICES = 32


def pair_table(key):
    base = jax.random.fold_in(key, 31)

    def single(index):
        return jax.random.permutation(jax.random.fold_in(base, index), RB_DEV * NTOUCH)[:NT_DEV]
    return jax.vmap(single)(jnp.arange(DEVICES)).reshape(-1).astype(jnp.int32)


def draw_tile_ray(key, part):
    return (pair_table(key) // NTOUCH).astype(jnp.int32)


def draw_tile_col(key, part):
    return (pair_table(key) % NTOUCH).astype(jnp.int32)


def region_layout(key):
    base = jax.random.fold_in(key, 53)
    groups = VBLOCKS // REGION

    def single(group):
        return jax.random.permutation(jax.random.fold_in(base, group), REGION)
    perms = jax.vmap(single)(jnp.arange(groups))
    home_map = (perms + (jnp.arange(groups) * REGION)[:, None]).reshape(-1).astype(jnp.int32)
    inverse = jnp.zeros((VBLOCKS,), jnp.int32).at[home_map].set(jnp.arange(VBLOCKS, dtype=jnp.int32))
    return (home_map, inverse)


def draw_home(key, part):
    return region_layout(key)[0]


def draw_touched(key, part):
    home_map, inverse = region_layout(key)
    base = jax.random.fold_in(key, 71)
    group_size = REGION // VBLK_DEV
    items = group_size * CAP

    def single(device):
        group = device // group_size
        hot = jax.random.randint(jax.random.fold_in(jax.random.fold_in(base, 1), group), (), 0, group_size)
        dev_key = jax.random.fold_in(jax.random.fold_in(base, 2), device)
        order = jax.random.permutation(jax.random.fold_in(dev_key, 0), items)
        score = jnp.zeros((items,), jnp.int32).at[order].set(jnp.arange(items, dtype=jnp.int32))
        item_ids = jnp.arange(items, dtype=jnp.int32)
        score = jnp.where(item_ids // CAP == hot, item_ids % CAP - CAP, score)
        chosen = jnp.argsort(score)[:NTOUCH]
        shuffle = jax.random.permutation(jax.random.fold_in(jax.random.fold_in(dev_key, 3), 0), NTOUCH)
        chosen = chosen[shuffle]
        row_key = jax.random.fold_in(dev_key, 5)
        local_rows = jax.vmap(lambda holder: jax.random.permutation(jax.random.fold_in(row_key, holder), VBLK_DEV)[:CAP])(jnp.arange(group_size))
        holder = chosen // CAP
        local = local_rows[holder, chosen % CAP]
        stored = group * REGION + holder * VBLK_DEV + local
        return inverse[stored]
    return jax.vmap(single)(jnp.arange(DEVICES)).reshape(-1).astype(jnp.int32)


def shard_levels(key, shape, cuts, low, top_value):
    def one(dim, blocks):
        steps = jax.random.uniform(jax.random.fold_in(jax.random.fold_in(key, 6), dim), (blocks,), jnp.float32, low / len(cuts), top_value / len(cuts))
        return jnp.repeat(jnp.exp(steps), shape[dim] // blocks).reshape((-1,) + (1,) * (len(shape) - dim - 1))

    level = one(*cuts[0])
    for cut in cuts[1:]:
        level = level * one(*cut)
    return level


def centred(stream_key, shape, scale, reach, split=(), held_as=jnp.bfloat16):
    array = scale * jax.random.normal(stream_key, shape, jnp.float32)
    if split:
        array = array * shard_levels(stream_key, shape, split, -0.22, 0.18)
    return jnp.clip(array, -reach, reach).astype(held_as)


def setup_inputs(seed: int = 0) -> dict:
    seeds = jax.random.split(jax.random.key(seed), 7)
    return {
        "tiles": centred(seeds[0], (TILES, BLK, BLK), (TILES_RB * BLK) ** -0.5, 0.125, ((0, 32),)),
        "tile_ray": draw_tile_ray(jax.random.fold_in(seeds[6], 71), 0),
        "tile_col": draw_tile_col(jax.random.fold_in(seeds[6], 71), 0),
        "touched": draw_touched(jax.random.fold_in(seeds[6], 71), 0),
        "home": draw_home(jax.random.fold_in(seeds[6], 71), 0),
        "sketch": centred(seeds[5], (VOX, K), 1.0, 6.0, ((0, 32),)),
    }


gram_shift = 0.001

def reference(tiles, tile_ray, tile_col, touched, home, sketch):
    tile_size = tiles.shape[1]
    width = sketch.shape[1]
    device = jnp.arange(TILES, dtype=jnp.int32) // NT_DEV
    ray_global = (device * RB_DEV + tile_ray).astype(jnp.int32)
    voxel_block = touched[(device * NTOUCH + tile_col).astype(jnp.int32)]
    position = home[voxel_block].astype(jnp.int32)
    sketch_blocks = sketch.reshape(VBLOCKS, tile_size, width)
    batch_rows = math.gcd(TILES, 512)
    rounds = TILES // batch_rows
    tile_steps = tiles.reshape(rounds, batch_rows, tile_size, tile_size)
    ray_steps = ray_global.reshape(rounds, batch_rows)
    pos_steps = position.reshape(rounds, batch_rows)

    def image_step(running, inputs):
        tile_block, ray_block, pos_block = inputs
        gathered = sketch_blocks[pos_block].astype(jnp.float32)
        product = jnp.einsum('tab,tbk->tak', tile_block.astype(jnp.float32), gathered, precision=lax.Precision.HIGHEST)
        return (running.at[ray_block].add(product), None)
    images, _ = lax.scan(image_step, jnp.zeros((RAYBLK, tile_size, width), jnp.float32), (tile_steps, ray_steps, pos_steps))
    images = images.astype(jnp.bfloat16)

    def normal_step(running, inputs):
        tile_block, ray_block, pos_block = inputs
        gathered = images[ray_block].astype(jnp.float32)
        product = jnp.einsum('tab,tak->tbk', tile_block.astype(jnp.float32), gathered, precision=lax.Precision.HIGHEST)
        return (running.at[pos_block].add(product), None)
    normal, _ = lax.scan(normal_step, jnp.zeros((VBLOCKS, tile_size, width), jnp.float32), (tile_steps, ray_steps, pos_steps))
    normal = normal.reshape(VOX, width)
    gram_matrix = jnp.dot(normal.T, normal, precision=lax.Precision.HIGHEST) / VOX + gram_shift * jnp.eye(width, dtype=jnp.float32)
    r_factor = jnp.linalg.cholesky(gram_matrix).T
    inverse = jax.scipy.linalg.solve_triangular(r_factor, jnp.eye(width, dtype=jnp.float32), lower=False)
    basis_out = jnp.dot(normal, inverse, precision=lax.Precision.HIGHEST)
    return (basis_out, r_factor)
```

```python
import functools

import jax
import jax.numpy as jnp
from jax import lax
from jax.experimental import pallas as pl
from jax.experimental.pallas import tpu as pltpu
from jax.sharding import PartitionSpec as P

CAP = 3
RB_DEV = 32


gram_shift = 0.001

MIB = 2**20
SMEM = pl.BlockSpec(memory_space=pltpu.SMEM)
VMEM = pl.BlockSpec(memory_space=pltpu.VMEM)
ANY = pl.BlockSpec(memory_space=pl.ANY)


def in_vmem(shape, dtype):
    return pltpu.VMEM(shape, dtype)


def plan_kernel(block_count, touched_ref, home_ref, request_ref, position_ref, used_ref):
    group_size = request_ref.shape[0]

    @pl.loop(0, group_size)
    def _(holder):
        used_ref[holder] = 0
        for slot in range(CAP):
            request_ref[holder, slot] = -1

    @pl.loop(0, touched_ref.shape[0])
    def _(entry):
        stored = home_ref[touched_ref[entry]]
        holder = lax.rem(lax.div(stored, block_count), group_size)
        slot = used_ref[holder]
        used_ref[holder] = slot + 1
        request_ref[holder, slot] = lax.rem(stored, block_count)
        position_ref[entry] = holder * CAP + slot


def serve_kernel(asked_ref, sketch_ref, served_ref, sem):
    slots, tile_size, width = served_ref.shape

    def copy(slot):
        row = jnp.maximum(asked_ref[lax.div(slot, CAP), lax.rem(slot, CAP)], 0)
        return pltpu.make_async_copy(sketch_ref.at[row], served_ref.at[slot], sem)

    @pl.loop(0, slots)
    def _(slot):
        copy(slot).start()

    pltpu.make_async_copy(served_ref, served_ref, sem).wait()


def load_kernel(ray_ref, col_ref, place_ref, tiles_ref, dense_ref, sem):
    count, tile_size, _ = tiles_ref.shape
    rows, cols = dense_ref.shape

    @pl.loop(0, rows // tile_size)
    def _(block):
        dense_ref[pl.ds(block * tile_size, tile_size), :] = jnp.zeros((tile_size, cols), dense_ref.dtype)

    @pl.loop(0, count)
    def _(tile):
        row = pl.multiple_of(ray_ref[tile] * tile_size, tile_size)
        col = pl.multiple_of(place_ref[col_ref[tile]] * tile_size, tile_size)
        pltpu.make_async_copy(
            tiles_ref.at[tile],
            dense_ref.at[pl.ds(row, tile_size), pl.ds(col, tile_size)],
            sem,
        ).start()

    filled = dense_ref.at[:, pl.ds(0, count * tile_size * tile_size // rows)]
    pltpu.make_async_copy(filled, filled, sem).wait()


def project_kernel(dense_ref, sketch_ref, part_ref, images_ref):
    rows, cols = dense_ref.shape
    step = 256

    @pl.loop(0, rows // step)
    def _(chunk):
        at = pl.multiple_of(chunk * step, step)
        image = jnp.dot(dense_ref[pl.ds(at, step), :], sketch_ref[...], preferred_element_type=jnp.float32)
        images_ref[:, pl.ds(at, step)] = image.astype(jnp.bfloat16).T

    @pl.loop(0, cols // step)
    def _(chunk):
        at = pl.multiple_of(chunk * step, step)
        part = jnp.dot(images_ref[...], dense_ref[:, pl.ds(at, step)], preferred_element_type=jnp.float32)
        part_ref[pl.ds(at, step), :] = part.T.astype(part_ref.dtype)


def zero_kernel(out_ref, zeros_ref, sem):
    rows = zeros_ref.shape[0]
    zeros_ref[...] = jnp.zeros(zeros_ref.shape, zeros_ref.dtype)

    @pl.loop(0, out_ref.shape[0] // rows)
    def _(chunk):
        pltpu.make_async_copy(zeros_ref, out_ref.at[pl.ds(chunk * rows, rows)], sem).start()

    pltpu.make_async_copy(out_ref, out_ref, sem).wait()


def split(value):
    high = value.astype(jnp.bfloat16)
    return high, (value - high.astype(jnp.float32)).astype(jnp.bfloat16)


def gather_kernel(asked_ref, arrived_ref, normal_ref, gram_ref, block_ref, seen_ref):
    slots, tile_size, width = arrived_ref.shape

    @pl.loop(0, seen_ref.shape[0])
    def _(row):
        seen_ref[row] = -1

    normal_ref[...] = jnp.zeros(normal_ref.shape, normal_ref.dtype)

    def place(slot, filled):
        row = asked_ref[lax.div(slot, CAP), lax.rem(slot, CAP)]
        safe = jnp.maximum(row, 0)
        known = seen_ref[safe]
        fresh = jnp.logical_and(row >= 0, known < 0)
        at = jnp.where(known < 0, filled, known)
        block_ref[slot] = -1

        @pl.when(row >= 0)
        def _():
            seen_ref[safe] = at
            block_ref[at] = safe
            normal_ref[at] += arrived_ref[slot].astype(jnp.float32)

        return jnp.where(fresh, filled + 1, filled)

    lax.fori_loop(0, slots, place, 0)

    gram_ref[...] = jnp.zeros(gram_ref.shape, gram_ref.dtype)

    @pl.loop(0, slots // CAP)
    def _(chunk):
        rows = jnp.concatenate([normal_ref[chunk * CAP + i] for i in range(CAP)], axis=0)
        high, low = split(rows)
        both = lax.dot_general(
            high, jnp.concatenate([high, low], axis=1), (((0,), (0,)), ((), ())),
            preferred_element_type=jnp.float32,
        )
        cross = both[:, width:]
        gram_ref[...] += both[:, :width] + cross + cross.T


def three(value):
    high = value.astype(jnp.bfloat16).astype(jnp.float32)
    rest = value - high
    mid = rest.astype(jnp.bfloat16).astype(jnp.float32)
    return high, mid, rest - mid


def finish_kernel(voxels, block_ref, gram_ref, normal_ref, zeroed_ref, basis_ref, factor_ref, work_ref, out_ref, sem):
    width = gram_ref.shape[0]
    slots, tile_size, _ = normal_ref.shape
    panel = 8
    row_at = lax.broadcasted_iota(jnp.int32, (width, width), 0)
    col_at = lax.broadcasted_iota(jnp.int32, (width, width), 1)
    unit = jnp.where(row_at == col_at, 1.0, 0.0).astype(jnp.float32)
    work_ref[:, :width] = gram_ref[...] / voxels + gram_shift * unit
    work_ref[:, width:] = unit
    in_panel = lax.broadcasted_iota(jnp.int32, (panel, 1), 0)
    for start in range(0, width, panel):
        rows = work_ref[pl.ds(start, panel), :]
        scale = jnp.zeros((panel, 1), jnp.float32)
        for k in range(panel):
            column = rows[:, start + k : start + k + 1]
            pivot = rows[k : k + 1, start + k : start + k + 1]
            rows = rows - jnp.where(in_panel > k, column / pivot, 0.0) * rows[k : k + 1, :]
            scale = jnp.where(in_panel == k, lax.rsqrt(pivot), scale)
        rows = rows * scale
        work_ref[pl.ds(start, panel), :] = rows
        if start + panel < width:
            high, mid, low = three(rows)
            left = jnp.concatenate([high, high, mid, high, low, mid], axis=0)[:, :width]
            right = jnp.concatenate([high, mid, high, low, high, mid], axis=0)
            update = lax.dot_general(
                left.astype(jnp.bfloat16), right.astype(jnp.bfloat16), (((0,), (0,)), ((), ())),
                preferred_element_type=jnp.float32,
            )
            work_ref[pl.ds(start + panel, width - start - panel), :] -= update[start + panel :, :]
    factor_ref[...] = jnp.where(col_at >= row_at, work_ref[:, :width], 0.0)
    inverse = jnp.where(col_at <= row_at, work_ref[:, width:], 0.0).T
    high, low = split(inverse)
    weights = jnp.concatenate([high, high, low], axis=0)

    @pl.loop(0, slots)
    def _(slot):
        row_high, row_low = split(normal_ref[slot])
        out_ref[slot] = jnp.dot(
            jnp.concatenate([row_high, row_low, row_high], axis=1), weights,
            preferred_element_type=jnp.float32,
        )

        @pl.when(block_ref[slot] >= 0)
        def _():
            at = block_ref[slot] * tile_size
            pltpu.make_async_copy(out_ref.at[slot], basis_ref.at[pl.ds(at, tile_size)], sem.at[slot]).start()

    @pl.loop(0, slots)
    def _(slot):
        @pl.when(block_ref[slot] >= 0)
        def _():
            at = block_ref[slot] * tile_size
            pltpu.make_async_copy(out_ref.at[slot], basis_ref.at[pl.ds(at, tile_size)], sem.at[slot]).wait()


def summed(value, axis):
    size = lax.axis_size(axis)
    step = 1
    while step < size:
        value = value + lax.ppermute(value, axis, [(i, i ^ step) for i in range(size)])
        step *= 2
    return value


def local(tiles, tile_ray, tile_col, touched, home, sketch):
    group_size = lax.axis_size("dev")
    tile_size = tiles.shape[1]
    width = sketch.shape[1]
    block_count = sketch.shape[0] // tile_size
    ntouch = touched.shape[0]
    slots = group_size * CAP
    voxels = sketch.shape[0] * lax.axis_size("grp") * group_size

    request, position = pl.pallas_call(
        functools.partial(plan_kernel, block_count),
        out_shape=(
            jax.ShapeDtypeStruct((group_size, CAP), jnp.int32),
            jax.ShapeDtypeStruct((ntouch,), jnp.int32),
        ),
        in_specs=[SMEM, SMEM],
        out_specs=(SMEM, SMEM),
        scratch_shapes=[pltpu.SMEM((group_size,), jnp.int32)],
        name="plan",
    )(touched, home)
    asked = lax.all_to_all(request, "dev", split_axis=0, concat_axis=0, tiled=True)
    served = pl.pallas_call(
        serve_kernel,
        out_shape=jax.ShapeDtypeStruct((slots, tile_size, width), sketch.dtype),
        in_specs=[SMEM, ANY],
        out_specs=ANY,
        scratch_shapes=[pltpu.SemaphoreType.DMA],
        name="serve",
    )(asked, sketch.reshape(block_count, tile_size, width))
    replies = lax.all_to_all(
        served.reshape(group_size, CAP, tile_size, width), "dev", split_axis=0, concat_axis=0, tiled=True
    ).reshape(slots, tile_size, width)

    whole = slots == ntouch
    place = position if whole else jnp.arange(ntouch, dtype=jnp.int32)
    dense = pl.pallas_call(
        load_kernel,
        out_shape=in_vmem((RB_DEV * tile_size, ntouch * tile_size), tiles.dtype),
        in_specs=[SMEM, SMEM, SMEM, ANY],
        out_specs=VMEM,
        scratch_shapes=[pltpu.SemaphoreType.DMA],
        compiler_params=pltpu.CompilerParams(vmem_limit_bytes=8 * MIB),
        name="load",
    )(tile_ray, tile_col, place, tiles)
    columns = replies if whole else jnp.take(replies, position, axis=0)
    part = pl.pallas_call(
        project_kernel,
        out_shape=jax.ShapeDtypeStruct((ntouch * tile_size, width), jnp.bfloat16),
        in_specs=[VMEM, VMEM],
        out_specs=VMEM,
        scratch_shapes=[pltpu.VMEM((width, RB_DEV * tile_size), jnp.bfloat16)],
        compiler_params=pltpu.CompilerParams(vmem_limit_bytes=16 * MIB),
        name="project",
    )(dense, columns.reshape(ntouch * tile_size, width))
    part = part.reshape(ntouch, tile_size, width)
    if not whole:
        part = jnp.zeros((slots, tile_size, width), part.dtype).at[position].set(part)
    arrived = lax.all_to_all(
        part.reshape(group_size, CAP, tile_size, width), "dev", split_axis=0, concat_axis=0, tiled=True
    ).reshape(slots, tile_size, width)

    zeroed = pl.pallas_call(
        zero_kernel,
        out_shape=jax.ShapeDtypeStruct(sketch.shape, jnp.float32),
        in_specs=[],
        out_specs=ANY,
        scratch_shapes=[pltpu.VMEM((sketch.shape[0] // 8, width), jnp.float32), pltpu.SemaphoreType.DMA],
        name="zeros",
    )()
    normal, gram, blocks = pl.pallas_call(
        gather_kernel,
        out_shape=(
            in_vmem((slots, tile_size, width), jnp.float32),
            jax.ShapeDtypeStruct((width, width), jnp.float32),
            jax.ShapeDtypeStruct((slots,), jnp.int32),
        ),
        in_specs=[SMEM, VMEM],
        out_specs=(VMEM, VMEM, SMEM),
        scratch_shapes=[pltpu.SMEM((block_count,), jnp.int32)],
        compiler_params=pltpu.CompilerParams(vmem_limit_bytes=16 * MIB),
        name="collect",
    )(asked, arrived)
    gram = summed(summed(gram, "grp"), "dev")
    return pl.pallas_call(
        functools.partial(finish_kernel, voxels),
        out_shape=(
            jax.ShapeDtypeStruct(sketch.shape, jnp.float32),
            jax.ShapeDtypeStruct((width, width), jnp.float32),
        ),
        in_specs=[SMEM, VMEM, VMEM, ANY],
        out_specs=(ANY, VMEM),
        scratch_shapes=[
            pltpu.VMEM((width, 2 * width), jnp.float32),
            pltpu.VMEM((slots, tile_size, width), jnp.float32),
            pltpu.SemaphoreType.DMA((slots,)),
        ],
        input_output_aliases={3: 0},
        compiler_params=pltpu.CompilerParams(vmem_limit_bytes=16 * MIB),
        name="finish",
    )(blocks, gram, normal, zeroed)


def solution(mesh):
    in_specs = (
        P(("grp", "dev"), None, None),
        P(("grp", "dev")),
        P(("grp", "dev")),
        P(("grp", "dev")),
        P(),
        P(("grp", "dev"), None),
    )
    out_specs = (P(("grp", "dev"), None), P())
    return jax.shard_map(local, mesh=mesh, in_specs=in_specs, out_specs=out_specs, check_vma=False)
```

```python
import functools

import jax
import jax.numpy as jnp
from jax import lax
from jax.experimental import pallas as pl
from jax.experimental.pallas import tpu as pltpu
from jax.sharding import PartitionSpec as P

CAP = 3
RB_DEV = 32


gram_shift = 0.001

MIB = 2**20
SMEM = pl.BlockSpec(memory_space=pltpu.SMEM)
VMEM = pl.BlockSpec(memory_space=pltpu.VMEM)
ANY = pl.BlockSpec(memory_space=pl.ANY)


def in_vmem(shape, dtype):
    return pltpu.VMEM(shape, dtype)


def held(value):
    return pltpu.with_memory_space_constraint(value, pltpu.VMEM)


def in_hbm(value):
    return pltpu.with_memory_space_constraint(value, pltpu.HBM)


def plan_kernel(block_count, touched_ref, home_ref, request_ref, position_ref, used_ref):
    group_size = request_ref.shape[0]

    @pl.loop(0, group_size)
    def _(holder):
        used_ref[holder] = 0
        for slot in range(CAP):
            request_ref[holder, slot] = -1

    @pl.loop(0, touched_ref.shape[0])
    def _(entry):
        stored = home_ref[touched_ref[entry]]
        holder = lax.rem(lax.div(stored, block_count), group_size)
        slot = used_ref[holder]
        used_ref[holder] = slot + 1
        request_ref[holder, slot] = lax.rem(stored, block_count)
        position_ref[entry] = holder * CAP + slot


def serve_kernel(asked_ref, sketch_ref, served_ref, sem):
    slots, tile_size, width = served_ref.shape

    def copy(slot):
        row = jnp.maximum(asked_ref[lax.div(slot, CAP), lax.rem(slot, CAP)], 0)
        return pltpu.make_async_copy(sketch_ref.at[row], served_ref.at[slot], sem)

    @pl.loop(0, slots)
    def _(slot):
        copy(slot).start()

    pltpu.make_async_copy(served_ref, served_ref, sem).wait()


def load_kernel(ray_ref, col_ref, place_ref, tiles_ref, dense_ref, sem):
    count, tile_size, _ = tiles_ref.shape
    rows, cols = dense_ref.shape

    @pl.loop(0, rows // tile_size)
    def _(block):
        dense_ref[pl.ds(block * tile_size, tile_size), :] = jnp.zeros((tile_size, cols), dense_ref.dtype)

    @pl.loop(0, count)
    def _(tile):
        row = pl.multiple_of(ray_ref[tile] * tile_size, tile_size)
        col = pl.multiple_of(place_ref[col_ref[tile]] * tile_size, tile_size)
        pltpu.make_async_copy(
            tiles_ref.at[tile],
            dense_ref.at[pl.ds(row, tile_size), pl.ds(col, tile_size)],
            sem,
        ).start()

    filled = dense_ref.at[:, pl.ds(0, count * tile_size * tile_size // rows)]
    pltpu.make_async_copy(filled, filled, sem).wait()


def project_kernel(dense_ref, sketch_ref, part_ref, images_ref):
    rows, cols = dense_ref.shape
    step = 256

    @pl.loop(0, rows // step)
    def _(chunk):
        at = pl.multiple_of(chunk * step, step)
        image = jnp.dot(dense_ref[pl.ds(at, step), :], sketch_ref[...], preferred_element_type=jnp.float32)
        images_ref[:, pl.ds(at, step)] = image.astype(jnp.bfloat16).T

    @pl.loop(0, cols // step)
    def _(chunk):
        at = pl.multiple_of(chunk * step, step)
        part = jnp.dot(images_ref[...], dense_ref[:, pl.ds(at, step)], preferred_element_type=jnp.float32)
        part_ref[pl.ds(at, step), :] = part.T.astype(part_ref.dtype)


def zero_kernel(out_ref, zeros_ref, sem):
    rows = zeros_ref.shape[0]
    zeros_ref[...] = jnp.zeros(zeros_ref.shape, zeros_ref.dtype)

    @pl.loop(0, out_ref.shape[0] // rows)
    def _(chunk):
        pltpu.make_async_copy(zeros_ref, out_ref.at[pl.ds(chunk * rows, rows)], sem).start()

    pltpu.make_async_copy(out_ref, out_ref, sem).wait()


def split(value):
    high = value.astype(jnp.bfloat16)
    return high, (value - high.astype(jnp.float32)).astype(jnp.bfloat16)


def gather_kernel(asked_ref, arrived_ref, normal_ref, gram_ref, block_ref, seen_ref):
    slots, tile_size, width = arrived_ref.shape

    @pl.loop(0, seen_ref.shape[0])
    def _(row):
        seen_ref[row] = -1

    normal_ref[...] = jnp.zeros(normal_ref.shape, normal_ref.dtype)

    def place(slot, filled):
        row = asked_ref[lax.div(slot, CAP), lax.rem(slot, CAP)]
        safe = jnp.maximum(row, 0)
        known = seen_ref[safe]
        fresh = jnp.logical_and(row >= 0, known < 0)
        at = jnp.where(known < 0, filled, known)
        block_ref[slot] = -1

        @pl.when(row >= 0)
        def _():
            seen_ref[safe] = at
            block_ref[at] = safe
            normal_ref[at] += arrived_ref[slot].astype(jnp.float32)

        return jnp.where(fresh, filled + 1, filled)

    lax.fori_loop(0, slots, place, 0)

    gram_ref[...] = jnp.zeros(gram_ref.shape, gram_ref.dtype)

    @pl.loop(0, slots // CAP)
    def _(chunk):
        rows = jnp.concatenate([normal_ref[chunk * CAP + i] for i in range(CAP)], axis=0)
        high, low = split(rows)
        both = lax.dot_general(
            high, jnp.concatenate([high, low], axis=1), (((0,), (0,)), ((), ())),
            preferred_element_type=jnp.float32,
        )
        cross = both[:, width:]
        gram_ref[...] += both[:, :width] + cross + cross.T


def spread(value, like):
    return jnp.broadcast_to(value, like.shape)


def factor(gram, inverse_ref):
    panel, width = gram[0].shape
    gram = list(gram)
    row_at = lax.broadcasted_iota(jnp.int32, (panel, width), 0)
    lane = lax.broadcasted_iota(jnp.int32, (panel, width), 1)
    right = [jnp.where(lane == row_at + panel * i, 1.0, 0.0) for i in range(len(gram))]
    upper = []
    for p in range(len(gram)):
        start = panel * p
        columns = [
            [spread(rows[:, start + k : start + k + 1], rows) for k in range(panel)] for rows in gram[p:]
        ]
        corner = list(columns[0])
        left_rows, right_rows = gram[p], right[p]
        upper_rows, inverse_rows = jnp.zeros_like(left_rows), jnp.zeros_like(left_rows)
        for k in range(panel):
            pivot = spread(corner[k][k : k + 1], left_rows)
            reciprocal, root = 1.0 / pivot, lax.rsqrt(pivot)
            here = row_at == k
            left_row, right_row = spread(left_rows[k : k + 1], left_rows), spread(right_rows[k : k + 1], left_rows)
            upper_rows = jnp.where(here, left_row * root, upper_rows)
            inverse_rows = jnp.where(here, right_row * root, inverse_rows)
            by = jnp.where(here, -1.0, corner[k])
            for j in range(k + 1, panel):
                scaled = spread(corner[j][k : k + 1], left_rows) * reciprocal
                corner[j] = jnp.where(here, 0.0, corner[j]) - by * scaled
            left_rows = jnp.where(here, 0.0, left_rows) - by * (left_row * reciprocal)
            right_rows = jnp.where(here, 0.0, right_rows) - by * (right_row * reciprocal)
        upper.append(jnp.where(lane >= row_at + start, upper_rows, 0.0))
        inverse_ref[pl.ds(start, panel), :] = jnp.where(lane <= row_at + start, inverse_rows, 0.0)
        left_each = [spread(left_rows[k : k + 1], left_rows) for k in range(panel)]
        right_each = [spread(right_rows[k : k + 1], left_rows) for k in range(panel)]
        for i in range(p + 1, len(gram)):
            by = columns[i - p]
            gram[i] = gram[i] - total([b * row for b, row in zip(by, left_each)])
            right[i] = right[i] - total([b * row for b, row in zip(by, right_each)])
    return upper


def total(terms):
    while len(terms) > 1:
        terms = [sum(terms[i + 1 : i + 2], terms[i]) for i in range(0, len(terms), 2)]
    return terms[0]


def finish_kernel(voxels, block_ref, gram_ref, normal_ref, zeroed_ref, basis_ref, factor_ref, work_ref, out_ref, sem):
    width = gram_ref.shape[0]
    slots, tile_size, _ = normal_ref.shape
    panel = 8
    row_at = lax.broadcasted_iota(jnp.int32, (panel, width), 0)
    lane = lax.broadcasted_iota(jnp.int32, (panel, width), 1)
    gram = []
    for start in range(0, width, panel):
        shift = jnp.where(lane == row_at + start, gram_shift, 0.0)
        gram.append(gram_ref[pl.ds(start, panel), :] / voxels + shift)
    for i, rows in enumerate(factor(gram, work_ref)):
        factor_ref[pl.ds(panel * i, panel), :] = rows
    inverse = work_ref[...].T
    high, low = split(inverse)
    weights = jnp.concatenate([high, high, low], axis=0)

    @pl.loop(0, slots)
    def _(slot):
        row_high, row_low = split(normal_ref[slot])
        out_ref[slot] = jnp.dot(
            jnp.concatenate([row_high, row_low, row_high], axis=1), weights,
            preferred_element_type=jnp.float32,
        )

        @pl.when(block_ref[slot] >= 0)
        def _():
            at = block_ref[slot] * tile_size
            pltpu.make_async_copy(out_ref.at[slot], basis_ref.at[pl.ds(at, tile_size)], sem.at[slot]).start()

    @pl.loop(0, slots)
    def _(slot):
        @pl.when(block_ref[slot] >= 0)
        def _():
            at = block_ref[slot] * tile_size
            pltpu.make_async_copy(out_ref.at[slot], basis_ref.at[pl.ds(at, tile_size)], sem.at[slot]).wait()


def summed(value, axis):
    size = lax.axis_size(axis)
    step = 1
    while step < size:
        value = value + lax.ppermute(value, axis, [(i, i ^ step) for i in range(size)])
        step *= 2
    return value


def local(tiles, tile_ray, tile_col, touched, home, sketch):
    group_size = lax.axis_size("dev")
    tile_size = tiles.shape[1]
    width = sketch.shape[1]
    block_count = sketch.shape[0] // tile_size
    ntouch = touched.shape[0]
    slots = group_size * CAP
    voxels = sketch.shape[0] * lax.axis_size("grp") * group_size

    request, position = pl.pallas_call(
        functools.partial(plan_kernel, block_count),
        out_shape=(
            jax.ShapeDtypeStruct((group_size, CAP), jnp.int32),
            jax.ShapeDtypeStruct((ntouch,), jnp.int32),
        ),
        in_specs=[SMEM, SMEM],
        out_specs=(SMEM, SMEM),
        scratch_shapes=[pltpu.SMEM((group_size,), jnp.int32)],
        name="plan",
    )(touched, home)
    asked = lax.all_to_all(request, "dev", split_axis=0, concat_axis=0, tiled=True)
    served = pl.pallas_call(
        serve_kernel,
        out_shape=jax.ShapeDtypeStruct((slots, tile_size, width), sketch.dtype),
        in_specs=[SMEM, ANY],
        out_specs=VMEM,
        scratch_shapes=[pltpu.SemaphoreType.DMA],
        name="serve",
    )(asked, in_hbm(sketch.reshape(block_count, tile_size, width)))
    replies = lax.all_to_all(
        served.reshape(group_size, CAP, tile_size, width), "dev", split_axis=0, concat_axis=0, tiled=True
    ).reshape(slots, tile_size, width)

    whole = slots == ntouch
    place = position if whole else jnp.arange(ntouch, dtype=jnp.int32)
    dense = pl.pallas_call(
        load_kernel,
        out_shape=in_vmem((RB_DEV * tile_size, ntouch * tile_size), tiles.dtype),
        in_specs=[SMEM, SMEM, SMEM, ANY],
        out_specs=VMEM,
        scratch_shapes=[pltpu.SemaphoreType.DMA],
        compiler_params=pltpu.CompilerParams(vmem_limit_bytes=8 * MIB),
        name="load",
    )(tile_ray, tile_col, place, in_hbm(tiles))
    columns = replies if whole else jnp.take(replies, position, axis=0)
    part = pl.pallas_call(
        project_kernel,
        out_shape=jax.ShapeDtypeStruct((ntouch * tile_size, width), jnp.bfloat16),
        in_specs=[VMEM, VMEM],
        out_specs=VMEM,
        scratch_shapes=[pltpu.VMEM((width, RB_DEV * tile_size), jnp.bfloat16)],
        compiler_params=pltpu.CompilerParams(vmem_limit_bytes=16 * MIB),
        name="project",
    )(held(dense), columns.reshape(ntouch * tile_size, width))
    part = part.reshape(ntouch, tile_size, width)
    if not whole:
        part = jnp.zeros((slots, tile_size, width), part.dtype).at[position].set(part)
    arrived = lax.all_to_all(
        part.reshape(group_size, CAP, tile_size, width), "dev", split_axis=0, concat_axis=0, tiled=True
    ).reshape(slots, tile_size, width)

    zeroed = pl.pallas_call(
        zero_kernel,
        out_shape=jax.ShapeDtypeStruct(sketch.shape, jnp.float32),
        in_specs=[],
        out_specs=ANY,
        scratch_shapes=[pltpu.VMEM((sketch.shape[0] // 8, width), jnp.float32), pltpu.SemaphoreType.DMA],
        name="zeros",
    )()
    normal, gram, blocks = pl.pallas_call(
        gather_kernel,
        out_shape=(
            in_vmem((slots, tile_size, width), jnp.float32),
            jax.ShapeDtypeStruct((width, width), jnp.float32),
            jax.ShapeDtypeStruct((slots,), jnp.int32),
        ),
        in_specs=[SMEM, VMEM],
        out_specs=(VMEM, VMEM, SMEM),
        scratch_shapes=[pltpu.SMEM((block_count,), jnp.int32)],
        compiler_params=pltpu.CompilerParams(vmem_limit_bytes=16 * MIB),
        name="collect",
    )(asked, arrived)
    gram = summed(summed(gram, "grp"), "dev")
    return pl.pallas_call(
        functools.partial(finish_kernel, voxels),
        out_shape=(
            jax.ShapeDtypeStruct(sketch.shape, jnp.float32),
            jax.ShapeDtypeStruct((width, width), jnp.float32),
        ),
        in_specs=[SMEM, VMEM, VMEM, ANY],
        out_specs=(ANY, VMEM),
        scratch_shapes=[
            pltpu.VMEM((width, width), jnp.float32),
            pltpu.VMEM((slots, tile_size, width), jnp.float32),
            pltpu.SemaphoreType.DMA((slots,)),
        ],
        input_output_aliases={3: 0},
        compiler_params=pltpu.CompilerParams(vmem_limit_bytes=16 * MIB),
        name="finish",
    )(blocks, gram, held(normal), zeroed)


def solution(mesh):
    in_specs = (
        P(("grp", "dev"), None, None),
        P(("grp", "dev")),
        P(("grp", "dev")),
        P(("grp", "dev")),
        P(),
        P(("grp", "dev"), None),
    )
    out_specs = (P(("grp", "dev"), None), P())
    return jax.shard_map(local, mesh=mesh, in_specs=in_specs, out_specs=out_specs, check_vma=False)
```

```python
import functools

import jax
import jax.numpy as jnp
from jax import lax
from jax.experimental import pallas as pl
from jax.experimental.pallas import tpu as pltpu
from jax.sharding import PartitionSpec as P

CAP = 3
RB_DEV = 32


gram_shift = 0.001

MIB = 2**20
IMAGE_STEP = 1024
PART_STEP = 768
SMEM = pl.BlockSpec(memory_space=pltpu.SMEM)
VMEM = pl.BlockSpec(memory_space=pltpu.VMEM)
ANY = pl.BlockSpec(memory_space=pl.ANY)


def in_vmem(shape, dtype):
    return pltpu.VMEM(shape, dtype)


def held(value):
    return pltpu.with_memory_space_constraint(value, pltpu.VMEM)


def in_hbm(value):
    return pltpu.with_memory_space_constraint(value, pltpu.HBM)


def plan_kernel(block_count, me_ref, touched_ref, home_ref, request_ref, place_ref, used_ref):
    group_size = request_ref.shape[0]

    @pl.loop(0, group_size)
    def _(holder):
        used_ref[holder] = 0
        for slot in range(CAP):
            request_ref[holder, slot] = -1

    @pl.loop(0, touched_ref.shape[0])
    def _(entry):
        stored = home_ref[touched_ref[entry]]
        holder = lax.rem(lax.div(stored, block_count), group_size)
        slot = used_ref[holder]
        used_ref[holder] = slot + 1
        request_ref[holder, slot] = lax.rem(stored, block_count)
        place_ref[entry] = jnp.bitwise_xor(holder, me_ref[0]) * CAP + slot


def serve_kernel(me_ref, asked_ref, _, sketch_ref, *refs):
    served_refs, sem = refs[:-1], refs[-1]

    for differs, served_ref in enumerate(served_refs):
        for slot in range(CAP):
            row = jnp.maximum(asked_ref[jnp.bitwise_xor(me_ref[0], differs), slot], 0)
            pltpu.make_async_copy(sketch_ref.at[row], served_ref.at[slot], sem).start()

    for served_ref in served_refs:
        pltpu.make_async_copy(served_ref, served_ref, sem).wait()


def table_kernel(ray_ref, col_ref, place_ref, table_ref):
    slots = table_ref.shape[0] // RB_DEV

    @pl.loop(0, table_ref.shape[0], unroll=8)
    def _(cell):
        table_ref[cell] = -1

    @pl.loop(0, ray_ref.shape[0], unroll=8)
    def _(tile):
        table_ref[ray_ref[tile] * slots + place_ref[col_ref[tile]]] = tile


def fill(first, table_ref, tiles_ref, dense_ref, blank_ref, sems):
    tile_size = tiles_ref.shape[1]
    rows, cols = dense_ref.shape
    some, slots = cols // tile_size, table_ref.shape[0] // (rows // tile_size)
    blank_ref[...] = jnp.zeros(blank_ref.shape, blank_ref.dtype)

    @pl.loop(0, rows // tile_size)
    def _(block):
        sem = sems.at[lax.div(block, IMAGE_STEP // tile_size)]
        row = pl.multiple_of(block * tile_size, tile_size)
        for slot in range(some):
            tile = table_ref[block * slots + first + slot]
            to = dense_ref.at[pl.ds(row, tile_size), slot * tile_size : (slot + 1) * tile_size]

            @pl.when(tile >= 0)
            def _(tile=tile, to=to):
                pltpu.make_async_copy(tiles_ref.at[tile], to, sem).start()

            @pl.when(tile < 0)
            def _(to=to):
                pltpu.make_async_copy(blank_ref, to, sem).start()


def filled(dense_ref, sems, chunk):
    rows = dense_ref.at[pl.ds(pl.multiple_of(chunk * IMAGE_STEP, IMAGE_STEP), IMAGE_STEP)]
    pltpu.make_async_copy(rows, rows, sems.at[chunk]).wait()


def stack(refs, stacked_ref, sem):
    copies, at = [], 0
    for ref in refs:
        for i in range(ref.shape[0]):
            to = stacked_ref.at[at : at + ref.shape[1]]
            copies.append(pltpu.make_async_copy(ref.at[i], to, sem))
            at += ref.shape[1]
    for copy in copies:
        copy.start()


def near_kernel(holders, table_ref, tiles_ref, *refs):
    sketch_refs, (sum_ref, dense_ref, blank_ref, sems, sketch_ref, sem) = refs[:holders], refs[holders:]
    stack(sketch_refs, sketch_ref, sem)
    fill(0, table_ref, tiles_ref, dense_ref, blank_ref, sems)
    pltpu.make_async_copy(sketch_ref, sketch_ref, sem).wait()

    @pl.loop(0, dense_ref.shape[0] // IMAGE_STEP)
    def _(chunk):
        filled(dense_ref, sems, chunk)
        rows = pl.ds(pl.multiple_of(chunk * IMAGE_STEP, IMAGE_STEP), IMAGE_STEP)
        sum_ref[rows, :] = jnp.dot(dense_ref[rows, :], sketch_ref[...], preferred_element_type=jnp.float32)


def parts(images_ref, dense_ref, part_refs):
    tall = part_refs[0].shape[0]
    each = PART_STEP // tall
    for first in range(0, len(part_refs), each):
        cols = dense_ref[:, first * tall : (first + each) * tall]
        part = jnp.dot(images_ref[...], cols, preferred_element_type=jnp.float32).T
        for i, part_ref in enumerate(part_refs[first : first + each]):
            part_ref[...] = part[i * tall : (i + 1) * tall].astype(part_ref.dtype)


def far_kernel(holders, table_ref, tiles_ref, sum_ref, *refs):
    sketch_refs, (token_ref, images_ref) = refs[:holders], refs[holders : holders + 2]
    part_refs, (dense_ref, blank_ref, sems, sketch_ref, sem) = refs[holders + 2 : -5], refs[-5:]
    token_ref[...] = jnp.zeros(token_ref.shape, token_ref.dtype)
    stack(sketch_refs, sketch_ref, sem)
    fill(holders * CAP, table_ref, tiles_ref, dense_ref, blank_ref, sems)
    pltpu.make_async_copy(sketch_ref, sketch_ref, sem).wait()

    @pl.loop(0, dense_ref.shape[0] // IMAGE_STEP)
    def _(chunk):
        filled(dense_ref, sems, chunk)
        rows = pl.ds(pl.multiple_of(chunk * IMAGE_STEP, IMAGE_STEP), IMAGE_STEP)
        image = sum_ref[rows, :] + jnp.dot(dense_ref[rows, :], sketch_ref[...], preferred_element_type=jnp.float32)
        images_ref[:, rows] = image.astype(jnp.bfloat16).T

    parts(images_ref, dense_ref, part_refs)


def rest_kernel(table_ref, tiles_ref, images_ref, _, *refs):
    part_refs, (dense_ref, blank_ref, sems) = refs[:-3], refs[-3:]
    fill(0, table_ref, tiles_ref, dense_ref, blank_ref, sems)

    @pl.loop(0, dense_ref.shape[0] // IMAGE_STEP)
    def _(chunk):
        filled(dense_ref, sems, chunk)

    parts(images_ref, dense_ref, part_refs)


def zero_kernel(out_ref, zeros_ref, sem):
    rows = zeros_ref.shape[0]
    zeros_ref[...] = jnp.zeros(zeros_ref.shape, zeros_ref.dtype)

    @pl.loop(0, out_ref.shape[0] // rows)
    def _(chunk):
        pltpu.make_async_copy(zeros_ref, out_ref.at[pl.ds(chunk * rows, rows)], sem).start()

    pltpu.make_async_copy(out_ref, out_ref, sem).wait()


def split(value):
    high = value.astype(jnp.bfloat16)
    return high, (value - high.astype(jnp.float32)).astype(jnp.bfloat16)


def gather_kernel(me_ref, asked_ref, *refs):
    arrived_refs, (normal_ref, gram_ref, block_ref, seen_ref) = refs[:-4], refs[-4:]
    slots, tile_size, width = normal_ref.shape

    @pl.loop(0, seen_ref.shape[0])
    def _(row):
        seen_ref[row] = -1

    @pl.loop(0, slots)
    def _(slot):
        block_ref[slot] = -1

    normal_ref[...] = jnp.zeros(normal_ref.shape, normal_ref.dtype)
    filled = 0
    for differs, arrived_ref in enumerate(arrived_refs):
        for slot in range(CAP):
            row = asked_ref[jnp.bitwise_xor(me_ref[0], differs), slot]
            safe = jnp.maximum(row, 0)
            known = seen_ref[safe]
            fresh = jnp.logical_and(row >= 0, known < 0)
            at = jnp.where(known < 0, filled, known)

            @pl.when(row >= 0)
            def _(at=at, safe=safe, arrived_ref=arrived_ref, slot=slot):
                seen_ref[safe] = at
                block_ref[at] = safe
                normal_ref[at] += arrived_ref[pl.ds(slot * tile_size, tile_size), :].astype(jnp.float32)

            filled = jnp.where(fresh, filled + 1, filled)

    gram_ref[...] = jnp.zeros(gram_ref.shape, gram_ref.dtype)

    @pl.loop(0, slots // CAP)
    def _(chunk):
        rows = jnp.concatenate([normal_ref[chunk * CAP + i] for i in range(CAP)], axis=0)
        high, low = split(rows)
        both = lax.dot_general(
            high, jnp.concatenate([high, low], axis=1), (((0,), (0,)), ((), ())),
            preferred_element_type=jnp.float32,
        )
        cross = both[:, width:]
        gram_ref[...] += both[:, :width] + cross + cross.T


def spread(value, like):
    return jnp.broadcast_to(value, like.shape)


def factor(gram, inverse_ref):
    panel, width = gram[0].shape
    gram = list(gram)
    row_at = lax.broadcasted_iota(jnp.int32, (panel, width), 0)
    lane = lax.broadcasted_iota(jnp.int32, (panel, width), 1)
    right = [jnp.where(lane == row_at + panel * i, 1.0, 0.0) for i in range(len(gram))]
    upper = []
    for p in range(len(gram)):
        start = panel * p
        columns = [
            [spread(rows[:, start + k : start + k + 1], rows) for k in range(panel)] for rows in gram[p:]
        ]
        corner = list(columns[0])
        left_rows, right_rows = gram[p], right[p]
        upper_rows, inverse_rows = jnp.zeros_like(left_rows), jnp.zeros_like(left_rows)
        for k in range(panel):
            pivot = spread(corner[k][k : k + 1], left_rows)
            reciprocal, root = 1.0 / pivot, lax.rsqrt(pivot)
            here = row_at == k
            left_row, right_row = spread(left_rows[k : k + 1], left_rows), spread(right_rows[k : k + 1], left_rows)
            upper_rows = jnp.where(here, left_row * root, upper_rows)
            inverse_rows = jnp.where(here, right_row * root, inverse_rows)
            by = jnp.where(here, -1.0, corner[k])
            for j in range(k + 1, panel):
                scaled = spread(corner[j][k : k + 1], left_rows) * reciprocal
                corner[j] = jnp.where(here, 0.0, corner[j]) - by * scaled
            left_rows = jnp.where(here, 0.0, left_rows) - by * (left_row * reciprocal)
            right_rows = jnp.where(here, 0.0, right_rows) - by * (right_row * reciprocal)
        upper.append(jnp.where(lane >= row_at + start, upper_rows, 0.0))
        inverse_ref[pl.ds(start, panel), :] = jnp.where(lane <= row_at + start, inverse_rows, 0.0)
        left_each = [spread(left_rows[k : k + 1], left_rows) for k in range(panel)]
        right_each = [spread(right_rows[k : k + 1], left_rows) for k in range(panel)]
        for i in range(p + 1, len(gram)):
            by = columns[i - p]
            gram[i] = gram[i] - total([b * row for b, row in zip(by, left_each)])
            right[i] = right[i] - total([b * row for b, row in zip(by, right_each)])
    return upper


def total(terms):
    while len(terms) > 1:
        terms = [sum(terms[i + 1 : i + 2], terms[i]) for i in range(0, len(terms), 2)]
    return terms[0]


def finish_kernel(voxels, block_ref, gram_ref, normal_ref, zeroed_ref, basis_ref, factor_ref, work_ref, out_ref, sem):
    width = gram_ref.shape[0]
    slots, tile_size, _ = normal_ref.shape
    panel = 8
    row_at = lax.broadcasted_iota(jnp.int32, (panel, width), 0)
    lane = lax.broadcasted_iota(jnp.int32, (panel, width), 1)
    gram = []
    for start in range(0, width, panel):
        shift = jnp.where(lane == row_at + start, gram_shift, 0.0)
        gram.append(gram_ref[pl.ds(start, panel), :] / voxels + shift)
    for i, rows in enumerate(factor(gram, work_ref)):
        factor_ref[pl.ds(panel * i, panel), :] = rows
    inverse = work_ref[...].T
    high, low = split(inverse)
    weights = jnp.concatenate([high, high, low], axis=0)

    @pl.loop(0, slots)
    def _(slot):
        row_high, row_low = split(normal_ref[slot])
        out_ref[slot] = jnp.dot(
            jnp.concatenate([row_high, row_low, row_high], axis=1), weights,
            preferred_element_type=jnp.float32,
        )

        @pl.when(block_ref[slot] >= 0)
        def _():
            at = block_ref[slot] * tile_size
            pltpu.make_async_copy(out_ref.at[slot], basis_ref.at[pl.ds(at, tile_size)], sem.at[slot]).start()

    @pl.loop(0, slots)
    def _(slot):
        @pl.when(block_ref[slot] >= 0)
        def _():
            at = block_ref[slot] * tile_size
            pltpu.make_async_copy(out_ref.at[slot], basis_ref.at[pl.ds(at, tile_size)], sem.at[slot]).wait()


def summed(value, axis):
    size = lax.axis_size(axis)
    step = 1
    while step < size:
        value = value + lax.ppermute(value, axis, [(i, i ^ step) for i in range(size)])
        step *= 2
    return value


def exchanged(values, first):
    size = lax.axis_size("dev")
    return [
        lax.ppermute(value, "dev", [(j, j ^ (first + i)) for j in range(size)]) for i, value in enumerate(values)
    ]


def local(tiles, tile_ray, tile_col, touched, home, sketch):
    group_size = lax.axis_size("dev")
    tile_size = tiles.shape[1]
    width = sketch.shape[1]
    block_count = sketch.shape[0] // tile_size
    ntouch = touched.shape[0]
    slots = group_size * CAP
    voxels = sketch.shape[0] * lax.axis_size("grp") * group_size

    half = group_size // 2
    rows, tall = RB_DEV * tile_size, CAP * tile_size
    me = lax.axis_index("dev").astype(jnp.int32).reshape(1)

    request, place = pl.pallas_call(
        functools.partial(plan_kernel, block_count),
        out_shape=(
            jax.ShapeDtypeStruct((group_size, CAP), jnp.int32),
            jax.ShapeDtypeStruct((ntouch,), jnp.int32),
        ),
        in_specs=[SMEM, SMEM, SMEM],
        out_specs=(SMEM, SMEM),
        scratch_shapes=[pltpu.SMEM((group_size,), jnp.int32)],
        name="plan",
    )(me, touched, home)
    table = pl.pallas_call(
        table_kernel,
        out_shape=jax.ShapeDtypeStruct((RB_DEV * slots,), jnp.int32),
        in_specs=[SMEM, SMEM, SMEM],
        out_specs=SMEM,
        name="table",
    )(tile_ray, tile_col, place)
    asked = lax.all_to_all(request, "dev", split_axis=0, concat_axis=0, tiled=True)
    served = pl.pallas_call(
        serve_kernel,
        out_shape=[jax.ShapeDtypeStruct((CAP, tile_size, width), sketch.dtype)] * group_size,
        in_specs=[SMEM, SMEM, ANY, ANY],
        out_specs=[VMEM] * group_size,
        scratch_shapes=[pltpu.SemaphoreType.DMA],
        name="serve",
    )(me, asked, table, in_hbm(sketch.reshape(block_count, tile_size, width)))
    replies = [served[0]] + exchanged(served[1:], 1)

    def with_tiles(kernel, outs, specs, operands, scratch, name, flops):
        return pl.pallas_call(
            kernel,
            out_shape=outs,
            in_specs=[SMEM, ANY] + specs,
            out_specs=[VMEM] * len(outs),
            scratch_shapes=[
                pltpu.VMEM((rows, half * tall), tiles.dtype),
                pltpu.VMEM((tile_size, tile_size), tiles.dtype),
                pltpu.SemaphoreType.DMA((rows // IMAGE_STEP,)),
            ]
            + scratch,
            compiler_params=pltpu.CompilerParams(vmem_limit_bytes=40 * MIB),
            cost_estimate=pl.CostEstimate(flops=flops, bytes_accessed=tiles.size, transcendentals=0),
            name=name,
        )(in_hbm(table), in_hbm(tiles), *operands)

    flops = 2 * rows * half * tall * width
    stacked = [pltpu.VMEM((half * tall, width), sketch.dtype), pltpu.SemaphoreType.DMA]
    (begun,) = with_tiles(
        functools.partial(near_kernel, half),
        [jax.ShapeDtypeStruct((rows, width), jnp.float32)],
        [ANY] * half,
        [in_hbm(block) for block in replies[:half]],
        stacked,
        "images_near",
        flops,
    )
    token, images, *far_parts = with_tiles(
        functools.partial(far_kernel, half),
        [
            jax.ShapeDtypeStruct((8, width), jnp.float32),
            jax.ShapeDtypeStruct((width, rows), jnp.bfloat16),
        ]
        + [jax.ShapeDtypeStruct((tall, width), jnp.bfloat16)] * half,
        [VMEM] + [ANY] * half,
        [begun] + [in_hbm(block) for block in replies[half:]],
        stacked,
        "images_far",
        2 * flops,
    )
    far_arrived = exchanged(far_parts, half)
    own_part, *near_parts = with_tiles(
        rest_kernel,
        [jax.ShapeDtypeStruct((tall, width), jnp.float32)]
        + [jax.ShapeDtypeStruct((tall, width), jnp.bfloat16)] * (half - 1),
        [VMEM, ANY],
        [images, exchanged([token], 1)[0]],
        [],
        "parts_near",
        flops,
    )
    arrived = [own_part] + exchanged(near_parts, 1) + far_arrived

    zeroed = pl.pallas_call(
        zero_kernel,
        out_shape=jax.ShapeDtypeStruct(sketch.shape, jnp.float32),
        in_specs=[],
        out_specs=ANY,
        scratch_shapes=[pltpu.VMEM((sketch.shape[0] // 8, width), jnp.float32), pltpu.SemaphoreType.DMA],
        name="zeros",
    )()
    normal, gram, blocks = pl.pallas_call(
        gather_kernel,
        out_shape=(
            in_vmem((slots, tile_size, width), jnp.float32),
            jax.ShapeDtypeStruct((width, width), jnp.float32),
            jax.ShapeDtypeStruct((slots,), jnp.int32),
        ),
        in_specs=[SMEM, SMEM] + [VMEM] * group_size,
        out_specs=(VMEM, VMEM, SMEM),
        scratch_shapes=[pltpu.SMEM((block_count,), jnp.int32)],
        compiler_params=pltpu.CompilerParams(vmem_limit_bytes=16 * MIB),
        name="collect",
    )(me, asked, *arrived)
    gram = summed(summed(gram, "grp"), "dev")
    return pl.pallas_call(
        functools.partial(finish_kernel, voxels),
        out_shape=(
            jax.ShapeDtypeStruct(sketch.shape, jnp.float32),
            jax.ShapeDtypeStruct((width, width), jnp.float32),
        ),
        in_specs=[SMEM, VMEM, VMEM, ANY],
        out_specs=(ANY, VMEM),
        scratch_shapes=[
            pltpu.VMEM((width, width), jnp.float32),
            pltpu.VMEM((slots, tile_size, width), jnp.float32),
            pltpu.SemaphoreType.DMA((slots,)),
        ],
        input_output_aliases={3: 0},
        compiler_params=pltpu.CompilerParams(vmem_limit_bytes=16 * MIB),
        name="finish",
    )(blocks, gram, held(normal), zeroed)


def solution(mesh):
    in_specs = (
        P(("grp", "dev"), None, None),
        P(("grp", "dev")),
        P(("grp", "dev")),
        P(("grp", "dev")),
        P(),
        P(("grp", "dev"), None),
    )
    out_specs = (P(("grp", "dev"), None), P())
    return jax.shard_map(local, mesh=mesh, in_specs=in_specs, out_specs=out_specs, check_vma=False)
```

```python
import functools

import jax
import jax.numpy as jnp
from jax import lax
from jax.experimental import pallas as pl
from jax.experimental.pallas import tpu as pltpu
from jax.sharding import PartitionSpec as P

CAP = 3
RB_DEV = 32


gram_shift = 0.001

MIB = 2**20
IMAGE_STEP = 1024
PART_STEP = 768
BASIS_SLOTS = 2 * CAP
SMEM = pl.BlockSpec(memory_space=pltpu.SMEM)
VMEM = pl.BlockSpec(memory_space=pltpu.VMEM)
ANY = pl.BlockSpec(memory_space=pl.ANY)


def in_vmem(shape, dtype):
    return pltpu.VMEM(shape, dtype)


def held(value):
    return pltpu.with_memory_space_constraint(value, pltpu.VMEM)


def in_hbm(value):
    return pltpu.with_memory_space_constraint(value, pltpu.HBM)


def plan_kernel(block_count, me_ref, touched_ref, home_ref, request_ref, place_ref, used_ref):
    group_size = request_ref.shape[0]

    @pl.loop(0, group_size)
    def _(holder):
        used_ref[holder] = 0
        for slot in range(CAP):
            request_ref[holder, slot] = -1

    @pl.loop(0, touched_ref.shape[0])
    def _(entry):
        stored = home_ref[touched_ref[entry]]
        holder = lax.rem(lax.div(stored, block_count), group_size)
        slot = used_ref[holder]
        used_ref[holder] = slot + 1
        request_ref[holder, slot] = lax.rem(stored, block_count)
        place_ref[entry] = jnp.bitwise_xor(holder, me_ref[0]) * CAP + slot


def serve_kernel(me_ref, asked_ref, sketch_ref, *refs):
    served_refs, sem = refs[:-1], refs[-1]

    for differs, served_ref in enumerate(served_refs):
        for slot in range(CAP):
            row = jnp.maximum(asked_ref[jnp.bitwise_xor(me_ref[0], differs), slot], 0)
            pltpu.make_async_copy(sketch_ref.at[row], served_ref.at[slot], sem).start()

    for served_ref in served_refs:
        pltpu.make_async_copy(served_ref, served_ref, sem).wait()


FIELD = 6
BUNCH = 4


def pack(tile, ray, slot):
    return lax.shift_left(lax.shift_left(tile, FIELD) + ray, FIELD) + slot


def unpack(entry):
    mask = 2**FIELD - 1
    cell = lax.shift_right_logical(entry, FIELD)
    return lax.shift_right_logical(cell, FIELD), jnp.bitwise_and(cell, mask), jnp.bitwise_and(entry, mask)


def list_kernel(chunks, slots, ray_ref, col_ref, place_ref, list_ref, count_ref):
    room = list_ref.shape[0] // (2 * chunks)
    rays, half = RB_DEV // chunks, slots // 2

    @pl.loop(0, 2 * chunks)
    def _(which):
        count_ref[which] = 0

    @pl.loop(0, ray_ref.shape[0], unroll=4)
    def _(tile):
        ray, slot = ray_ref[tile], place_ref[col_ref[tile]]
        far = (slot >= half).astype(jnp.int32)
        which = far * chunks + lax.div(ray, rays)
        count = count_ref[which]
        list_ref[which * room + count] = pack(tile, ray, slot - far * half)
        count_ref[which] = count + 1

    @pl.loop(0, 2 * chunks)
    def _(which):
        for _ in range(BUNCH - 1):
            count = count_ref[which]

            @pl.when(jnp.bitwise_and(count, BUNCH - 1) != 0)
            def _(count=count):
                list_ref[which * room + count] = RB_DEV << FIELD
                count_ref[which] = count + 1


def fill(far, list_ref, count_ref, tiles_ref, dense_ref, sems):
    tile_size = tiles_ref.shape[1]
    rows, cols = dense_ref.shape[0] - tile_size, dense_ref.shape[1]
    chunks = rows // IMAGE_STEP
    room = list_ref.shape[0] // (2 * chunks)

    @pl.loop(0, rows // tile_size)
    def _(block):
        at = pl.multiple_of(block * tile_size, tile_size)
        dense_ref[pl.ds(at, tile_size), :] = jnp.zeros((tile_size, cols), dense_ref.dtype)

    for chunk in range(chunks):
        which = far * chunks + chunk

        @pl.loop(0, lax.shift_right_logical(count_ref[which], BUNCH.bit_length() - 1))
        def _(bunch, which=which, chunk=chunk):
            entries = [list_ref[which * room + bunch * BUNCH + i] for i in range(BUNCH)]
            for tile, ray, slot in map(unpack, entries):
                row = pl.multiple_of(ray * tile_size, tile_size)
                col = pl.multiple_of(slot * tile_size, tile_size)
                to = dense_ref.at[pl.ds(row, tile_size), pl.ds(col, tile_size)]
                pltpu.make_async_copy(tiles_ref.at[tile], to, sems.at[chunk]).start()


def filled(far, count_ref, tiles_ref, sems, chunk):
    count = count_ref[far * sems.shape[0] + chunk]
    size = 1
    while size <= tiles_ref.shape[0]:

        @pl.when(jnp.bitwise_and(count, size) != 0)
        def _(size=size):
            some = tiles_ref.at[:size]
            pltpu.make_async_copy(some, some, sems.at[chunk]).wait()

        size *= 2


def stack(refs, stacked_ref, sem):
    copies, at = [], 0
    for ref in refs:
        for i in range(ref.shape[0]):
            to = stacked_ref.at[at : at + ref.shape[1]]
            copies.append(pltpu.make_async_copy(ref.at[i], to, sem))
            at += ref.shape[1]
    for copy in copies:
        copy.start()


def load_kernel(ray_ref, col_ref, place_ref, tiles_ref, _, dense_ref, sem):
    count, tile_size, _ = tiles_ref.shape
    rows, cols = dense_ref.shape

    @pl.loop(0, rows // tile_size)
    def _(block):
        at = pl.multiple_of(block * tile_size, tile_size)
        dense_ref[pl.ds(at, tile_size), :] = jnp.zeros((tile_size, cols), dense_ref.dtype)

    @pl.loop(0, count, unroll=8)
    def _(tile):
        row = pl.multiple_of(ray_ref[tile] * tile_size, tile_size)
        col = pl.multiple_of(place_ref[col_ref[tile]] * tile_size, tile_size)
        to = dense_ref.at[pl.ds(row, tile_size), pl.ds(col, tile_size)]
        pltpu.make_async_copy(tiles_ref.at[tile], to, sem).start()

    pltpu.make_async_copy(tiles_ref, tiles_ref, sem).wait()


def half_of(far, kept, refs):
    if kept:
        dense_ref, *refs = refs
        cols = dense_ref.shape[1] // 2
        return dense_ref.at[:, far * cols : (far + 1) * cols], lambda chunk: None, refs
    list_ref, count_ref, tiles_ref, *refs = refs
    *refs, dense_ref, sems = refs
    fill(far, list_ref, count_ref, tiles_ref, dense_ref, sems)
    return dense_ref, functools.partial(filled, far, count_ref, tiles_ref, sems), refs


def near_kernel(kept, *refs):
    dense_ref, ready, refs = half_of(0, kept, refs)
    *sketch_refs, sum_ref, sketch_ref, sem = refs
    stack(sketch_refs, sketch_ref, sem)
    pltpu.make_async_copy(sketch_ref, sketch_ref, sem).wait()

    @pl.loop(0, sum_ref.shape[0] // IMAGE_STEP)
    def _(chunk):
        ready(chunk)
        rows = pl.ds(pl.multiple_of(chunk * IMAGE_STEP, IMAGE_STEP), IMAGE_STEP)
        sum_ref[rows, :] = jnp.dot(dense_ref[rows, :], sketch_ref[...], preferred_element_type=jnp.float32)


def hand_out(total, part_refs):
    tall = part_refs[0].shape[0]
    for i, part_ref in enumerate(part_refs):
        part_ref[...] = total[:, i * tall : (i + 1) * tall].T.astype(part_ref.dtype)


def parts(images_ref, dense_ref, part_refs):
    rows, tall = images_ref.shape[1], part_refs[0].shape[0]
    each = PART_STEP // tall
    for first in range(0, len(part_refs), each):
        cols = dense_ref[:rows, first * tall : (first + each) * tall]
        part = jnp.dot(images_ref[...], cols, preferred_element_type=jnp.float32)
        hand_out(part, part_refs[first : first + each])


def far_kernel(holders, kept, *refs):
    dense_ref, ready, refs = half_of(1, kept, refs)
    sum_ref, *refs = refs
    sketch_refs, (token_ref, images_ref) = refs[:holders], refs[holders : holders + 2]
    *part_refs, sketch_ref, sem = refs[holders + 2 :]
    token_ref[...] = jnp.zeros(token_ref.shape, token_ref.dtype)
    stack(sketch_refs, sketch_ref, sem)
    pltpu.make_async_copy(sketch_ref, sketch_ref, sem).wait()

    @pl.loop(0, sum_ref.shape[0] // IMAGE_STEP)
    def _(chunk):
        ready(chunk)
        rows = pl.ds(pl.multiple_of(chunk * IMAGE_STEP, IMAGE_STEP), IMAGE_STEP)
        image = sum_ref[rows, :] + jnp.dot(dense_ref[rows, :], sketch_ref[...], preferred_element_type=jnp.float32)
        images_ref[:, rows] = image.astype(jnp.bfloat16).T

    parts(images_ref, dense_ref, part_refs)


def rest_kernel(kept, *refs):
    dense_ref, ready, refs = half_of(0, kept, refs)
    images_ref, _, *part_refs = refs

    @pl.loop(0, images_ref.shape[1] // IMAGE_STEP)
    def _(chunk):
        ready(chunk)

    parts(images_ref, dense_ref, part_refs)


def zero_kernel(out_ref, zeros_ref, sem):
    rows = zeros_ref.shape[0]
    zeros_ref[...] = jnp.zeros(zeros_ref.shape, zeros_ref.dtype)

    @pl.loop(0, out_ref.shape[0] // rows)
    def _(chunk):
        pltpu.make_async_copy(zeros_ref, out_ref.at[pl.ds(chunk * rows, rows)], sem).start()

    pltpu.make_async_copy(out_ref, out_ref, sem).wait()


def split(value):
    high = value.astype(jnp.bfloat16)
    return high, (value - high.astype(jnp.float32)).astype(jnp.bfloat16)


def gather_kernel(me_ref, asked_ref, *refs):
    arrived_refs, (split_ref, gram_ref, block_ref, normal_ref, seen_ref) = refs[:-5], refs[-5:]
    slots, tile_size, width = normal_ref.shape

    @pl.loop(0, seen_ref.shape[0])
    def _(row):
        seen_ref[row] = -1

    @pl.loop(0, slots)
    def _(slot):
        block_ref[slot] = -1

    normal_ref[...] = jnp.zeros(normal_ref.shape, normal_ref.dtype)
    filled = 0
    for differs, arrived_ref in enumerate(arrived_refs):
        for slot in range(CAP):
            row = asked_ref[jnp.bitwise_xor(me_ref[0], differs), slot]
            safe = jnp.maximum(row, 0)
            known = seen_ref[safe]
            fresh = jnp.logical_and(row >= 0, known < 0)
            at = jnp.where(known < 0, filled, known)

            @pl.when(row >= 0)
            def _(at=at, safe=safe, arrived_ref=arrived_ref, slot=slot):
                seen_ref[safe] = at
                block_ref[at] = safe
                normal_ref[at] += arrived_ref[pl.ds(slot * tile_size, tile_size), :].astype(jnp.float32)

            filled = jnp.where(fresh, filled + 1, filled)

    gram_ref[...] = jnp.zeros(gram_ref.shape, gram_ref.dtype)
    tall = BASIS_SLOTS * tile_size

    @pl.loop(0, slots // BASIS_SLOTS)
    def _(chunk):
        at = pl.multiple_of(chunk * tall, tall)
        rows = jnp.concatenate([normal_ref[chunk * BASIS_SLOTS + i] for i in range(BASIS_SLOTS)], axis=0)
        high, low = split(rows)
        both_rows = jnp.concatenate([high, low], axis=1)
        split_ref[pl.ds(at, tall), :] = both_rows
        both = lax.dot_general(high, both_rows, (((0,), (0,)), ((), ())), preferred_element_type=jnp.float32)
        cross = both[:, width:]
        gram_ref[...] += both[:, :width] + cross + cross.T


def spread(value, like):
    return jnp.broadcast_to(value, like.shape)


def factor(gram, inverse_ref):
    panel, width = gram[0].shape
    gram = list(gram)
    row_at = lax.broadcasted_iota(jnp.int32, (panel, width), 0)
    lane = lax.broadcasted_iota(jnp.int32, (panel, width), 1)
    right = [jnp.where(lane == row_at + panel * i, 1.0, 0.0) for i in range(len(gram))]
    upper = []
    for p in range(len(gram)):
        start = panel * p
        columns = [
            [spread(rows[:, start + k : start + k + 1], rows) for k in range(panel)] for rows in gram[p:]
        ]
        corner = list(columns[0])
        left_rows, right_rows = gram[p], right[p]
        upper_rows, inverse_rows = jnp.zeros_like(left_rows), jnp.zeros_like(left_rows)
        for k in range(panel):
            pivot = spread(corner[k][k : k + 1], left_rows)
            reciprocal, root = 1.0 / pivot, lax.rsqrt(pivot)
            here = row_at == k
            left_row, right_row = spread(left_rows[k : k + 1], left_rows), spread(right_rows[k : k + 1], left_rows)
            upper_rows = jnp.where(here, left_row * root, upper_rows)
            inverse_rows = jnp.where(here, right_row * root, inverse_rows)
            by = jnp.where(here, -1.0, corner[k])
            for j in range(k + 1, panel):
                scaled = spread(corner[j][k : k + 1], left_rows) * reciprocal
                corner[j] = jnp.where(here, 0.0, corner[j]) - by * scaled
            left_rows = jnp.where(here, 0.0, left_rows) - by * (left_row * reciprocal)
            right_rows = jnp.where(here, 0.0, right_rows) - by * (right_row * reciprocal)
        upper.append(jnp.where(lane >= row_at + start, upper_rows, 0.0))
        inverse_ref[pl.ds(start, panel), :] = jnp.where(lane <= row_at + start, inverse_rows, 0.0)
        left_each = [spread(left_rows[k : k + 1], left_rows) for k in range(panel)]
        right_each = [spread(right_rows[k : k + 1], left_rows) for k in range(panel)]
        for i in range(p + 1, len(gram)):
            by = columns[i - p]
            gram[i] = gram[i] - total([b * row for b, row in zip(by, left_each)])
            right[i] = right[i] - total([b * row for b, row in zip(by, right_each)])
    return upper


def total(terms):
    while len(terms) > 1:
        terms = [sum(terms[i + 1 : i + 2], terms[i]) for i in range(0, len(terms), 2)]
    return terms[0]


def finish_kernel(voxels, block_ref, gram_ref, normal_ref, zeroed_ref, basis_ref, factor_ref, work_ref, out_ref, sem):
    width = gram_ref.shape[0]
    slots, tile_size, _ = out_ref.shape
    panel = 8
    row_at = lax.broadcasted_iota(jnp.int32, (panel, width), 0)
    lane = lax.broadcasted_iota(jnp.int32, (panel, width), 1)
    gram = []
    for start in range(0, width, panel):
        shift = jnp.where(lane == row_at + start, gram_shift, 0.0)
        gram.append(gram_ref[pl.ds(start, panel), :] / voxels + shift)
    for i, rows in enumerate(factor(gram, work_ref)):
        factor_ref[pl.ds(panel * i, panel), :] = rows
    inverse = work_ref[...].T
    high, low = split(inverse)
    twice = jnp.concatenate([high, high], axis=0)
    tall = BASIS_SLOTS * tile_size

    def copy(slot):
        at = pl.multiple_of(block_ref[slot] * tile_size, tile_size)
        return pltpu.make_async_copy(out_ref.at[slot], basis_ref.at[pl.ds(at, tile_size)], sem.at[slot])

    @pl.loop(0, slots // BASIS_SLOTS)
    def _(chunk):
        rows = pl.ds(pl.multiple_of(chunk * tall, tall), tall)
        both = normal_ref[rows, :]
        value = jnp.dot(both, twice, preferred_element_type=jnp.float32)
        value += jnp.dot(both[:, :width], low, preferred_element_type=jnp.float32)
        for i in range(BASIS_SLOTS):
            slot = chunk * BASIS_SLOTS + i
            out_ref[slot] = value[i * tile_size : (i + 1) * tile_size]

            @pl.when(block_ref[slot] >= 0)
            def _(slot=slot):
                copy(slot).start()

    @pl.loop(0, slots)
    def _(slot):
        @pl.when(block_ref[slot] >= 0)
        def _():
            copy(slot).wait()


def summed(value, axes):
    outer, inner = (lax.axis_size(axis) for axis in axes)

    def other(bits):
        return lax.ppermute(value, axes, [(i, i ^ bits) for i in range(outer * inner)])

    def powers(low, high):
        return [1 << i for i in range(low.bit_length() - 1, high.bit_length() - 1)]

    core, *rest = powers(inner, outer * inner)
    near = powers(1, inner)
    odd = len(near) % 2
    bits = near[:odd] + rest + near[odd:]
    value = value + other(core)
    for i in range(0, len(bits) - 1, 2):
        one, two = bits[i : i + 2]
        value = (value + other(one)) + (other(two) + other(one ^ two))
    if len(bits) % 2:
        value = value + other(bits[-1])
    return value


def exchanged(values, first):
    size = lax.axis_size("dev")
    return [
        lax.ppermute(value, "dev", [(j, j ^ (first + i)) for j in range(size)]) for i, value in enumerate(values)
    ]


def local(tiles, tile_ray, tile_col, touched, home, sketch):
    group_size = lax.axis_size("dev")
    tile_size = tiles.shape[1]
    width = sketch.shape[1]
    block_count = sketch.shape[0] // tile_size
    ntouch = touched.shape[0]
    slots = group_size * CAP
    voxels = sketch.shape[0] * lax.axis_size("grp") * group_size

    half = group_size // 2
    rows, tall = RB_DEV * tile_size, CAP * tile_size
    me = lax.axis_index("dev").astype(jnp.int32).reshape(1)

    request, place = pl.pallas_call(
        functools.partial(plan_kernel, block_count),
        out_shape=(
            jax.ShapeDtypeStruct((group_size, CAP), jnp.int32),
            jax.ShapeDtypeStruct((ntouch,), jnp.int32),
        ),
        in_specs=[SMEM, SMEM, SMEM],
        out_specs=(SMEM, SMEM),
        scratch_shapes=[pltpu.SMEM((group_size,), jnp.int32)],
        name="plan",
    )(me, touched, home)
    kept = rows * slots * tile_size * tiles.dtype.itemsize <= 24 * MIB
    chunks = rows // IMAGE_STEP
    if not kept:
        room = min(RB_DEV // chunks * slots // 2, tiles.shape[0] + BUNCH)
        listed, counts = pl.pallas_call(
            functools.partial(list_kernel, chunks, slots),
            out_shape=(
                jax.ShapeDtypeStruct((2 * chunks * room,), jnp.int32),
                jax.ShapeDtypeStruct((2 * chunks,), jnp.int32),
            ),
            in_specs=[SMEM, SMEM, SMEM],
            out_specs=(SMEM, SMEM),
            name="list",
        )(tile_ray, tile_col, place)
        tile_operands, tile_specs = [listed, counts, in_hbm(tiles)], [SMEM, SMEM, ANY]
        tile_scratch = [
            pltpu.VMEM((rows + tile_size, half * tall), tiles.dtype),
            pltpu.SemaphoreType.DMA((chunks,)),
        ]
    asked = held(lax.all_to_all(request, "dev", split_axis=0, concat_axis=0, tiled=True))
    served = pl.pallas_call(
        serve_kernel,
        out_shape=[in_vmem((CAP, tile_size, width), sketch.dtype)] * group_size,
        in_specs=[SMEM, SMEM, ANY],
        out_specs=[VMEM] * group_size,
        scratch_shapes=[pltpu.SemaphoreType.DMA],
        compiler_params=pltpu.CompilerParams(vmem_limit_bytes=8 * MIB),
        name="serve",
    )(me, asked, in_hbm(sketch.reshape(block_count, tile_size, width)))
    replies = [served[0]] + exchanged(served[1:], 1)

    if kept:
        dense = pl.pallas_call(
            load_kernel,
            out_shape=in_vmem((rows, slots * tile_size), tiles.dtype),
            in_specs=[SMEM, SMEM, SMEM, ANY, ANY],
            out_specs=VMEM,
            scratch_shapes=[pltpu.SemaphoreType.DMA],
            compiler_params=pltpu.CompilerParams(vmem_limit_bytes=8 * MIB),
            name="load",
        )(in_hbm(tile_ray), in_hbm(tile_col), in_hbm(place), in_hbm(tiles), served[0])
        tile_operands, tile_specs, tile_scratch = [held(dense)], [VMEM], []

    def with_tiles(kernel, outs, specs, operands, scratch, name, flops):
        return pl.pallas_call(
            functools.partial(kernel, kept),
            out_shape=outs,
            in_specs=tile_specs + specs,
            out_specs=[VMEM] * len(outs),
            scratch_shapes=scratch + tile_scratch,
            compiler_params=pltpu.CompilerParams(vmem_limit_bytes=(12 if kept else 40) * MIB),
            cost_estimate=pl.CostEstimate(flops=flops, bytes_accessed=tiles.size, transcendentals=0),
            name=name,
        )(*tile_operands, *operands)

    flops = 2 * rows * half * tall * width
    stacked = [pltpu.VMEM((half * tall, width), sketch.dtype), pltpu.SemaphoreType.DMA]
    (begun,) = with_tiles(
        near_kernel,
        [jax.ShapeDtypeStruct((rows, width), jnp.float32)],
        [ANY] * half,
        replies[:half],
        stacked,
        "images_near",
        flops,
    )
    token, images, *far_parts = with_tiles(
        functools.partial(far_kernel, half),
        [
            jax.ShapeDtypeStruct((8, width), jnp.float32),
            jax.ShapeDtypeStruct((width, rows), jnp.bfloat16),
        ]
        + [jax.ShapeDtypeStruct((tall, width), jnp.bfloat16)] * half,
        [VMEM] + [ANY] * half,
        [begun] + replies[half:],
        stacked,
        "images_far",
        2 * flops,
    )
    far_arrived = exchanged(far_parts, half)
    own_part, *near_parts = with_tiles(
        rest_kernel,
        [jax.ShapeDtypeStruct((tall, width), jnp.float32)]
        + [jax.ShapeDtypeStruct((tall, width), jnp.bfloat16)] * (half - 1),
        [VMEM, ANY],
        [images, exchanged([token], 1)[0]],
        [],
        "parts_near",
        flops,
    )
    arrived = [own_part] + exchanged(near_parts, 1) + far_arrived

    zeroed = pl.pallas_call(
        zero_kernel,
        out_shape=jax.ShapeDtypeStruct(sketch.shape, jnp.float32),
        in_specs=[],
        out_specs=ANY,
        scratch_shapes=[pltpu.VMEM((sketch.shape[0] // 8, width), jnp.float32), pltpu.SemaphoreType.DMA],
        name="zeros",
    )()
    normal, gram, blocks = pl.pallas_call(
        gather_kernel,
        out_shape=(
            in_vmem((slots * tile_size, 2 * width), jnp.bfloat16),
            jax.ShapeDtypeStruct((width, width), jnp.float32),
            jax.ShapeDtypeStruct((slots,), jnp.int32),
        ),
        in_specs=[SMEM, SMEM] + [VMEM] * group_size,
        out_specs=(VMEM, VMEM, SMEM),
        scratch_shapes=[
            pltpu.VMEM((slots, tile_size, width), jnp.float32),
            pltpu.SMEM((block_count,), jnp.int32),
        ],
        compiler_params=pltpu.CompilerParams(vmem_limit_bytes=16 * MIB),
        name="collect",
    )(me, asked, *arrived)
    gram = summed(gram, ("grp", "dev"))
    return pl.pallas_call(
        functools.partial(finish_kernel, voxels),
        out_shape=(
            jax.ShapeDtypeStruct(sketch.shape, jnp.float32),
            jax.ShapeDtypeStruct((width, width), jnp.float32),
        ),
        in_specs=[SMEM, VMEM, VMEM, ANY],
        out_specs=(ANY, VMEM),
        scratch_shapes=[
            pltpu.VMEM((width, width), jnp.float32),
            pltpu.VMEM((slots, tile_size, width), jnp.float32),
            pltpu.SemaphoreType.DMA((slots,)),
        ],
        input_output_aliases={3: 0},
        compiler_params=pltpu.CompilerParams(vmem_limit_bytes=16 * MIB),
        name="finish",
    )(blocks, gram, held(normal), zeroed)


def solution(mesh):
    in_specs = (
        P(("grp", "dev"), None, None),
        P(("grp", "dev")),
        P(("grp", "dev")),
        P(("grp", "dev")),
        P(),
        P(("grp", "dev"), None),
    )
    out_specs = (P(("grp", "dev"), None), P())
    return jax.shard_map(local, mesh=mesh, in_specs=in_specs, out_specs=out_specs, check_vma=False)
```

```python
import functools

import jax
import jax.numpy as jnp
from jax import lax
from jax.experimental import pallas as pl
from jax.experimental.pallas import tpu as pltpu
from jax.sharding import PartitionSpec as P

CAP = 3
RB_DEV = 32


gram_shift = 0.001

MIB = 2**20
IMAGE_STEP = 1024
PART_STEP = 768
LATE = 2
PACK_SPARE = 8
BASIS_SLOTS = 2 * CAP
SMEM = pl.BlockSpec(memory_space=pltpu.SMEM)
VMEM = pl.BlockSpec(memory_space=pltpu.VMEM)
ANY = pl.BlockSpec(memory_space=pl.ANY)


def in_vmem(shape, dtype):
    return pltpu.VMEM(shape, dtype)


def held(value):
    return pltpu.with_memory_space_constraint(value, pltpu.VMEM)


def in_hbm(value):
    return pltpu.with_memory_space_constraint(value, pltpu.HBM)


def plan_kernel(block_count, me_ref, touched_ref, home_ref, request_ref, place_ref, used_ref):
    group_size = request_ref.shape[0]

    @pl.loop(0, group_size)
    def _(holder):
        used_ref[holder] = 0
        for slot in range(CAP):
            request_ref[holder, slot] = -1

    @pl.loop(0, touched_ref.shape[0])
    def _(entry):
        stored = home_ref[touched_ref[entry]]
        holder = lax.rem(lax.div(stored, block_count), group_size)
        slot = used_ref[holder]
        used_ref[holder] = slot + 1
        request_ref[holder, slot] = lax.rem(stored, block_count)
        place_ref[entry] = jnp.bitwise_xor(holder, me_ref[0]) * CAP + slot


def serve_kernel(me_ref, asked_ref, sketch_ref, *refs):
    served_refs, sem = refs[:-1], refs[-1]

    for differs, served_ref in enumerate(served_refs):
        for slot in range(CAP):
            row = jnp.maximum(asked_ref[jnp.bitwise_xor(me_ref[0], differs), slot], 0)
            pltpu.make_async_copy(sketch_ref.at[row], served_ref.at[slot], sem).start()

    for served_ref in served_refs:
        pltpu.make_async_copy(served_ref, served_ref, sem).wait()


FIELD = 6
BUNCH = 4


def pack(tile, ray, slot):
    return lax.shift_left(lax.shift_left(tile, FIELD) + ray, FIELD) + slot


def unpack(entry):
    mask = 2**FIELD - 1
    cell = lax.shift_right_logical(entry, FIELD)
    return lax.shift_right_logical(cell, FIELD), jnp.bitwise_and(cell, mask), jnp.bitwise_and(entry, mask)


def list_kernel(chunks, slots, ray_ref, col_ref, place_ref, list_ref, count_ref):
    room = list_ref.shape[0] // (2 * chunks)
    rays, half = RB_DEV // chunks, slots // 2

    @pl.loop(0, 2 * chunks)
    def _(which):
        count_ref[which] = 0

    @pl.loop(0, ray_ref.shape[0], unroll=4)
    def _(tile):
        ray, slot = ray_ref[tile], place_ref[col_ref[tile]]
        far = (slot >= half).astype(jnp.int32)
        which = far * chunks + lax.div(ray, rays)
        count = count_ref[which]
        list_ref[which * room + count] = pack(tile, ray, slot - far * half)
        count_ref[which] = count + 1

    @pl.loop(0, 2 * chunks)
    def _(which):
        for _ in range(BUNCH - 1):
            count = count_ref[which]

            @pl.when(jnp.bitwise_and(count, BUNCH - 1) != 0)
            def _(count=count):
                list_ref[which * room + count] = RB_DEV << FIELD
                count_ref[which] = count + 1


def fill(far, list_ref, count_ref, tiles_ref, dense_ref, sems):
    tile_size = tiles_ref.shape[1]
    rows, cols = dense_ref.shape[0] - tile_size, dense_ref.shape[1]
    chunks = rows // IMAGE_STEP
    room = list_ref.shape[0] // (2 * chunks)

    @pl.loop(0, rows // tile_size)
    def _(block):
        at = pl.multiple_of(block * tile_size, tile_size)
        dense_ref[pl.ds(at, tile_size), :] = jnp.zeros((tile_size, cols), dense_ref.dtype)

    for chunk in range(chunks):
        which = far * chunks + chunk

        @pl.loop(0, lax.shift_right_logical(count_ref[which], BUNCH.bit_length() - 1))
        def _(bunch, which=which, chunk=chunk):
            entries = [list_ref[which * room + bunch * BUNCH + i] for i in range(BUNCH)]
            for tile, ray, slot in map(unpack, entries):
                row = pl.multiple_of(ray * tile_size, tile_size)
                col = pl.multiple_of(slot * tile_size, tile_size)
                to = dense_ref.at[pl.ds(row, tile_size), pl.ds(col, tile_size)]
                pltpu.make_async_copy(tiles_ref.at[tile], to, sems.at[chunk]).start()


def filled(far, count_ref, tiles_ref, sems, chunk):
    count = count_ref[far * sems.shape[0] + chunk]
    size = 1
    while size <= tiles_ref.shape[0]:

        @pl.when(jnp.bitwise_and(count, size) != 0)
        def _(size=size):
            some = tiles_ref.at[:size]
            pltpu.make_async_copy(some, some, sems.at[chunk]).wait()

        size *= 2


def stack(refs, stacked_ref, sem):
    copies, at = [], 0
    for ref in refs:
        for i in range(ref.shape[0]):
            to = stacked_ref.at[at : at + ref.shape[1]]
            copies.append(pltpu.make_async_copy(ref.at[i], to, sem))
            at += ref.shape[1]
    for copy in copies:
        copy.start()


def load_kernel(ray_ref, col_ref, place_ref, tiles_ref, _, dense_ref, sem):
    count, tile_size, _ = tiles_ref.shape
    rows, cols = dense_ref.shape

    @pl.loop(0, rows // tile_size)
    def _(block):
        at = pl.multiple_of(block * tile_size, tile_size)
        dense_ref[pl.ds(at, tile_size), :] = jnp.zeros((tile_size, cols), dense_ref.dtype)

    @pl.loop(0, count, unroll=8)
    def _(tile):
        row = pl.multiple_of(ray_ref[tile] * tile_size, tile_size)
        col = pl.multiple_of(place_ref[col_ref[tile]] * tile_size, tile_size)
        to = dense_ref.at[pl.ds(row, tile_size), pl.ds(col, tile_size)]
        pltpu.make_async_copy(tiles_ref.at[tile], to, sem).start()

    pltpu.make_async_copy(tiles_ref, tiles_ref, sem).wait()


def half_of(far, kept, refs):
    if kept:
        dense_ref, *refs = refs
        cols = dense_ref.shape[1] // 2
        return dense_ref.at[:, far * cols : (far + 1) * cols], lambda chunk: None, refs
    list_ref, count_ref, tiles_ref, *refs = refs
    *refs, dense_ref, sems = refs
    fill(far, list_ref, count_ref, tiles_ref, dense_ref, sems)
    return dense_ref, functools.partial(filled, far, count_ref, tiles_ref, sems), refs


def near_kernel(kept, *refs):
    dense_ref, ready, refs = half_of(0, kept, refs)
    *sketch_refs, sum_ref, sketch_ref, sem = refs
    stack(sketch_refs, sketch_ref, sem)
    pltpu.make_async_copy(sketch_ref, sketch_ref, sem).wait()

    @pl.loop(0, sum_ref.shape[0] // IMAGE_STEP)
    def _(chunk):
        ready(chunk)
        rows = pl.ds(pl.multiple_of(chunk * IMAGE_STEP, IMAGE_STEP), IMAGE_STEP)
        sum_ref[rows, :] = jnp.dot(dense_ref[rows, :], sketch_ref[...], preferred_element_type=jnp.float32)


def hand_out(total, part_refs):
    tall = part_refs[0].shape[0]
    for i, part_ref in enumerate(part_refs):
        part_ref[...] = total[:, i * tall : (i + 1) * tall].T.astype(part_ref.dtype)


def parts(images_ref, dense_ref, part_refs):
    rows, tall = images_ref.shape[1], part_refs[0].shape[0]
    each = PART_STEP // tall
    for first in range(0, len(part_refs), each):
        cols = dense_ref[:rows, first * tall : (first + each) * tall]
        part = jnp.dot(images_ref[...], cols, preferred_element_type=jnp.float32)
        hand_out(part, part_refs[first : first + each])


def far_kernel(holders, late, kept, *refs):
    dense_ref, ready, refs = half_of(1, kept, refs)
    sum_ref, *refs = refs
    sketch_refs, (token_ref, images_ref) = refs[:holders], refs[holders : holders + 2]
    *part_refs, sketch_ref, sem = refs[holders + 2 :]
    token_ref[...] = jnp.zeros(token_ref.shape, token_ref.dtype)
    stack(sketch_refs, sketch_ref, sem)
    pltpu.make_async_copy(sketch_ref, sketch_ref, sem).wait()

    @pl.loop(0, sum_ref.shape[0] // IMAGE_STEP)
    def _(chunk):
        ready(chunk)
        rows = pl.ds(pl.multiple_of(chunk * IMAGE_STEP, IMAGE_STEP), IMAGE_STEP)
        image = sum_ref[rows, :] + jnp.dot(dense_ref[rows, :], sketch_ref[...], preferred_element_type=jnp.float32)
        images_ref[:, rows] = image.astype(jnp.bfloat16).T

    parts(images_ref, dense_ref, part_refs)


def rest_kernel(late, kept, *refs):
    all_ref = refs[0]
    dense_ref, ready, refs = half_of(0, kept, refs)
    images_ref, _, *part_refs = refs

    @pl.loop(0, images_ref.shape[1] // IMAGE_STEP)
    def _(chunk):
        ready(chunk)

    parts(images_ref, dense_ref, part_refs[: len(part_refs) - late])
    if late:
        first = all_ref.shape[1] - late * part_refs[0].shape[0]
        parts(images_ref, all_ref.at[:, first:], part_refs[len(part_refs) - late :])


def zero_kernel(out_ref, zeros_ref, sem):
    rows = zeros_ref.shape[0]
    zeros_ref[...] = jnp.zeros(zeros_ref.shape, zeros_ref.dtype)

    @pl.loop(0, out_ref.shape[0] // rows)
    def _(chunk):
        pltpu.make_async_copy(zeros_ref, out_ref.at[pl.ds(chunk * rows, rows)], sem).start()

    pltpu.make_async_copy(out_ref, out_ref, sem).wait()


def split(value):
    high = value.astype(jnp.bfloat16)
    return high, (value - high.astype(jnp.float32)).astype(jnp.bfloat16)


def gather_kernel(me_ref, asked_ref, *refs):
    arrived_refs, (split_ref, pack_ref, block_ref, normal_ref, gram_ref, seen_ref) = refs[:-6], refs[-6:]
    slots, tile_size, width = normal_ref.shape

    @pl.loop(0, seen_ref.shape[0])
    def _(row):
        seen_ref[row] = -1

    @pl.loop(0, slots)
    def _(slot):
        block_ref[slot] = -1

    normal_ref[...] = jnp.zeros(normal_ref.shape, normal_ref.dtype)
    filled = 0
    for differs, arrived_ref in enumerate(arrived_refs):
        for slot in range(CAP):
            row = asked_ref[jnp.bitwise_xor(me_ref[0], differs), slot]
            safe = jnp.maximum(row, 0)
            known = seen_ref[safe]
            fresh = jnp.logical_and(row >= 0, known < 0)
            at = jnp.where(known < 0, filled, known)

            @pl.when(row >= 0)
            def _(at=at, safe=safe, arrived_ref=arrived_ref, slot=slot):
                seen_ref[safe] = at
                block_ref[at] = safe
                normal_ref[at] += arrived_ref[pl.ds(slot * tile_size, tile_size), :].astype(jnp.float32)

            filled = jnp.where(fresh, filled + 1, filled)

    gram_ref[...] = jnp.zeros(gram_ref.shape, gram_ref.dtype)
    tall = BASIS_SLOTS * tile_size

    @pl.loop(0, slots // BASIS_SLOTS)
    def _(chunk):
        at = pl.multiple_of(chunk * tall, tall)
        rows = jnp.concatenate([normal_ref[chunk * BASIS_SLOTS + i] for i in range(BASIS_SLOTS)], axis=0)
        high, low = split(rows)
        both_rows = jnp.concatenate([high, low], axis=1)
        split_ref[pl.ds(at, tall), :] = both_rows
        both = lax.dot_general(high, both_rows, (((0,), (0,)), ((), ())), preferred_element_type=jnp.float32)
        cross = both[:, width:]
        gram_ref[...] += both[:, :width] + cross + cross.T

    pack_ref[...] = packed(gram_ref[...])


def packed(gram):
    half = gram.shape[0] // 2
    top, bottom = gram[:half], pltpu.roll(gram[half:], half, 1)
    row = lax.broadcasted_iota(jnp.int32, top.shape, 0)
    col = lax.broadcasted_iota(jnp.int32, top.shape, 1)
    diagonal = jnp.sum(jnp.where(col == row, bottom, 0.0), axis=0, keepdims=True)
    last = jnp.broadcast_to(diagonal, (PACK_SPARE, gram.shape[1]))
    return jnp.concatenate([jnp.where(col >= row, top, bottom), last], axis=0)


def unpacked(pack):
    half = pack.shape[0] - PACK_SPARE
    top, diagonal = pack[:half], pack[half : half + 1]
    row = lax.broadcasted_iota(jnp.int32, top.shape, 0)
    col = lax.broadcasted_iota(jnp.int32, top.shape, 1)
    low = jnp.where(col < row, top, jnp.where(col == row, diagonal, 0.0))
    turned = jnp.concatenate([low, jnp.zeros_like(low)], axis=0).T[:half]
    upper = jnp.concatenate([jnp.where(col >= row, top, 0.0), pltpu.roll(turned, half, 1)], axis=0)
    row = lax.broadcasted_iota(jnp.int32, upper.shape, 0)
    col = lax.broadcasted_iota(jnp.int32, upper.shape, 1)
    return upper + jnp.where(col > row, upper, 0.0).T


def spread(value, like):
    return jnp.broadcast_to(value, like.shape)


def factor(gram, inverse_ref):
    panel, width = gram[0].shape
    gram = list(gram)
    row_at = lax.broadcasted_iota(jnp.int32, (panel, width), 0)
    lane = lax.broadcasted_iota(jnp.int32, (panel, width), 1)
    right = [jnp.where(lane == row_at + panel * i, 1.0, 0.0) for i in range(len(gram))]
    upper = []
    for p in range(len(gram)):
        start = panel * p
        columns = [
            [spread(rows[:, start + k : start + k + 1], rows) for k in range(panel)] for rows in gram[p:]
        ]
        corner = list(columns[0])
        left_rows, right_rows = gram[p], right[p]
        upper_rows, inverse_rows = jnp.zeros_like(left_rows), jnp.zeros_like(left_rows)
        for k in range(panel):
            pivot = spread(corner[k][k : k + 1], left_rows)
            reciprocal, root = 1.0 / pivot, lax.rsqrt(pivot)
            here = row_at == k
            left_row, right_row = spread(left_rows[k : k + 1], left_rows), spread(right_rows[k : k + 1], left_rows)
            upper_rows = jnp.where(here, left_row * root, upper_rows)
            inverse_rows = jnp.where(here, right_row * root, inverse_rows)
            by = jnp.where(here, -1.0, corner[k])
            for j in range(k + 1, panel):
                scaled = spread(corner[j][k : k + 1], left_rows) * reciprocal
                corner[j] = jnp.where(here, 0.0, corner[j]) - by * scaled
            left_rows = jnp.where(here, 0.0, left_rows) - by * (left_row * reciprocal)
            right_rows = jnp.where(here, 0.0, right_rows) - by * (right_row * reciprocal)
        upper.append(jnp.where(lane >= row_at + start, upper_rows, 0.0))
        inverse_ref[pl.ds(start, panel), :] = jnp.where(lane <= row_at + start, inverse_rows, 0.0)
        left_each = [spread(left_rows[k : k + 1], left_rows) for k in range(panel)]
        right_each = [spread(right_rows[k : k + 1], left_rows) for k in range(panel)]
        for i in range(p + 1, len(gram)):
            by = columns[i - p]
            gram[i] = gram[i] - total([b * row for b, row in zip(by, left_each)])
            right[i] = right[i] - total([b * row for b, row in zip(by, right_each)])
    return upper


def total(terms):
    while len(terms) > 1:
        terms = [sum(terms[i + 1 : i + 2], terms[i]) for i in range(0, len(terms), 2)]
    return terms[0]


def finish_kernel(voxels, block_ref, pack_ref, normal_ref, zeroed_ref, basis_ref, factor_ref, work_ref, out_ref, sem):
    width = factor_ref.shape[0]
    slots, tile_size, _ = out_ref.shape
    panel = 8
    row_at = lax.broadcasted_iota(jnp.int32, (panel, width), 0)
    lane = lax.broadcasted_iota(jnp.int32, (panel, width), 1)
    whole = unpacked(pack_ref[...])
    gram = []
    for start in range(0, width, panel):
        shift = jnp.where(lane == row_at + start, gram_shift, 0.0)
        gram.append(whole[start : start + panel] / voxels + shift)
    for i, rows in enumerate(factor(gram, work_ref)):
        factor_ref[pl.ds(panel * i, panel), :] = rows
    inverse = work_ref[...].T
    high, low = split(inverse)
    twice = jnp.concatenate([high, high], axis=0)
    tall = BASIS_SLOTS * tile_size

    def copy(slot):
        at = pl.multiple_of(block_ref[slot] * tile_size, tile_size)
        return pltpu.make_async_copy(out_ref.at[slot], basis_ref.at[pl.ds(at, tile_size)], sem.at[slot])

    @pl.loop(0, slots // BASIS_SLOTS)
    def _(chunk):
        rows = pl.ds(pl.multiple_of(chunk * tall, tall), tall)
        both = normal_ref[rows, :]
        value = jnp.dot(both, twice, preferred_element_type=jnp.float32)
        value += jnp.dot(both[:, :width], low, preferred_element_type=jnp.float32)
        for i in range(BASIS_SLOTS):
            slot = chunk * BASIS_SLOTS + i
            out_ref[slot] = value[i * tile_size : (i + 1) * tile_size]

            @pl.when(block_ref[slot] >= 0)
            def _(slot=slot):
                copy(slot).start()

    @pl.loop(0, slots)
    def _(slot):
        @pl.when(block_ref[slot] >= 0)
        def _():
            copy(slot).wait()


def summed(value, axes):
    outer, inner = (lax.axis_size(axis) for axis in axes)

    def other(bits):
        return lax.ppermute(value, axes, [(i, i ^ bits) for i in range(outer * inner)])

    def powers(low, high):
        return [1 << i for i in range(low.bit_length() - 1, high.bit_length() - 1)]

    core, *rest = powers(inner, outer * inner)
    near = powers(1, inner)
    odd = len(near) % 2
    bits = near[:odd] + rest + near[odd:]
    value = value + other(core)
    for i in range(0, len(bits) - 1, 2):
        one, two = bits[i : i + 2]
        value = (value + other(one)) + (other(two) + other(one ^ two))
    if len(bits) % 2:
        value = value + other(bits[-1])
    return value


def exchanged(values, first):
    size = lax.axis_size("dev")
    return [
        lax.ppermute(value, "dev", [(j, j ^ (first + i)) for j in range(size)]) for i, value in enumerate(values)
    ]


def local(tiles, tile_ray, tile_col, touched, home, sketch):
    group_size = lax.axis_size("dev")
    tile_size = tiles.shape[1]
    width = sketch.shape[1]
    block_count = sketch.shape[0] // tile_size
    ntouch = touched.shape[0]
    slots = group_size * CAP
    voxels = sketch.shape[0] * lax.axis_size("grp") * group_size

    half = group_size // 2
    rows, tall = RB_DEV * tile_size, CAP * tile_size
    me = lax.axis_index("dev").astype(jnp.int32).reshape(1)

    request, place = pl.pallas_call(
        functools.partial(plan_kernel, block_count),
        out_shape=(
            jax.ShapeDtypeStruct((group_size, CAP), jnp.int32),
            jax.ShapeDtypeStruct((ntouch,), jnp.int32),
        ),
        in_specs=[SMEM, SMEM, SMEM],
        out_specs=(SMEM, SMEM),
        scratch_shapes=[pltpu.SMEM((group_size,), jnp.int32)],
        name="plan",
    )(me, touched, home)
    kept = rows * slots * tile_size * tiles.dtype.itemsize <= 24 * MIB
    chunks = rows // IMAGE_STEP
    if not kept:
        room = min(RB_DEV // chunks * slots // 2, tiles.shape[0] + BUNCH)
        listed, counts = pl.pallas_call(
            functools.partial(list_kernel, chunks, slots),
            out_shape=(
                jax.ShapeDtypeStruct((2 * chunks * room,), jnp.int32),
                jax.ShapeDtypeStruct((2 * chunks,), jnp.int32),
            ),
            in_specs=[SMEM, SMEM, SMEM],
            out_specs=(SMEM, SMEM),
            name="list",
        )(tile_ray, tile_col, place)
        tile_operands, tile_specs = [listed, counts, in_hbm(tiles)], [SMEM, SMEM, ANY]
        tile_scratch = [
            pltpu.VMEM((rows + tile_size, half * tall), tiles.dtype),
            pltpu.SemaphoreType.DMA((chunks,)),
        ]
    asked = held(lax.all_to_all(request, "dev", split_axis=0, concat_axis=0, tiled=True))
    served = pl.pallas_call(
        serve_kernel,
        out_shape=[in_vmem((CAP, tile_size, width), sketch.dtype)] * group_size,
        in_specs=[SMEM, SMEM, ANY],
        out_specs=[VMEM] * group_size,
        scratch_shapes=[pltpu.SemaphoreType.DMA],
        compiler_params=pltpu.CompilerParams(vmem_limit_bytes=8 * MIB),
        name="serve",
    )(me, asked, in_hbm(sketch.reshape(block_count, tile_size, width)))
    replies = [served[0]] + exchanged(served[1:], 1)

    if kept:
        dense = pl.pallas_call(
            load_kernel,
            out_shape=in_vmem((rows, slots * tile_size), tiles.dtype),
            in_specs=[SMEM, SMEM, SMEM, ANY, ANY],
            out_specs=VMEM,
            scratch_shapes=[pltpu.SemaphoreType.DMA],
            compiler_params=pltpu.CompilerParams(vmem_limit_bytes=8 * MIB),
            name="load",
        )(in_hbm(tile_ray), in_hbm(tile_col), in_hbm(place), in_hbm(tiles), served[0])
        tile_operands, tile_specs, tile_scratch = [held(dense)], [VMEM], []

    def with_tiles(kernel, outs, specs, operands, scratch, name, flops):
        return pl.pallas_call(
            functools.partial(kernel, kept),
            out_shape=outs,
            in_specs=tile_specs + specs,
            out_specs=[VMEM] * len(outs),
            scratch_shapes=scratch + tile_scratch,
            compiler_params=pltpu.CompilerParams(vmem_limit_bytes=(12 if kept else 40) * MIB),
            cost_estimate=pl.CostEstimate(flops=flops, bytes_accessed=tiles.size, transcendentals=0),
            name=name,
        )(*tile_operands, *operands)

    late = LATE if kept else 0
    flops = 2 * rows * half * tall * width
    stacked = [pltpu.VMEM((half * tall, width), sketch.dtype), pltpu.SemaphoreType.DMA]
    (begun,) = with_tiles(
        near_kernel,
        [jax.ShapeDtypeStruct((rows, width), jnp.float32)],
        [ANY] * half,
        replies[:half],
        stacked,
        "images_near",
        flops,
    )
    token, images, *far_parts = with_tiles(
        functools.partial(far_kernel, half, late),
        [
            jax.ShapeDtypeStruct((8, width), jnp.float32),
            jax.ShapeDtypeStruct((width, rows), jnp.bfloat16),
        ]
        + [jax.ShapeDtypeStruct((tall, width), jnp.bfloat16)] * (half - late),
        [VMEM] + [ANY] * half,
        [begun] + replies[half:],
        stacked,
        "images_far",
        2 * flops,
    )
    far_arrived = exchanged(far_parts, half)
    own_part, *near_parts = with_tiles(
        functools.partial(rest_kernel, late),
        [jax.ShapeDtypeStruct((tall, width), jnp.float32)]
        + [jax.ShapeDtypeStruct((tall, width), jnp.bfloat16)] * (half - 1 + late),
        [VMEM, ANY],
        [images, exchanged([token], 1)[0]],
        [],
        "parts_near",
        flops,
    )
    far_arrived += exchanged(near_parts[half - 1 :], group_size - late)
    arrived = [own_part] + exchanged(near_parts[: half - 1], 1) + far_arrived

    zeroed = pl.pallas_call(
        zero_kernel,
        out_shape=jax.ShapeDtypeStruct(sketch.shape, jnp.float32),
        in_specs=[],
        out_specs=ANY,
        scratch_shapes=[pltpu.VMEM((sketch.shape[0] // 8, width), jnp.float32), pltpu.SemaphoreType.DMA],
        name="zeros",
    )()
    normal, gram, blocks = pl.pallas_call(
        gather_kernel,
        out_shape=(
            in_vmem((slots * tile_size, 2 * width), jnp.bfloat16),
            jax.ShapeDtypeStruct((width // 2 + PACK_SPARE, width), jnp.float32),
            jax.ShapeDtypeStruct((slots,), jnp.int32),
        ),
        in_specs=[SMEM, SMEM] + [VMEM] * group_size,
        out_specs=(VMEM, VMEM, SMEM),
        scratch_shapes=[
            pltpu.VMEM((slots, tile_size, width), jnp.float32),
            pltpu.VMEM((width, width), jnp.float32),
            pltpu.SMEM((block_count,), jnp.int32),
        ],
        compiler_params=pltpu.CompilerParams(vmem_limit_bytes=16 * MIB),
        name="collect",
    )(me, asked, *arrived)
    gram = summed(gram, ("grp", "dev"))
    return pl.pallas_call(
        functools.partial(finish_kernel, voxels),
        out_shape=(
            jax.ShapeDtypeStruct(sketch.shape, jnp.float32),
            jax.ShapeDtypeStruct((width, width), jnp.float32),
        ),
        in_specs=[SMEM, VMEM, VMEM, ANY],
        out_specs=(ANY, VMEM),
        scratch_shapes=[
            pltpu.VMEM((width, width), jnp.float32),
            pltpu.VMEM((slots, tile_size, width), jnp.float32),
            pltpu.SemaphoreType.DMA((slots,)),
        ],
        input_output_aliases={3: 0},
        compiler_params=pltpu.CompilerParams(vmem_limit_bytes=16 * MIB),
        name="finish",
    )(blocks, gram, held(normal), zeroed)


def solution(mesh):
    in_specs = (
        P(("grp", "dev"), None, None),
        P(("grp", "dev")),
        P(("grp", "dev")),
        P(("grp", "dev")),
        P(),
        P(("grp", "dev"), None),
    )
    out_specs = (P(("grp", "dev"), None), P())
    return jax.shard_map(local, mesh=mesh, in_specs=in_specs, out_specs=out_specs, check_vma=False)
```

```python
import functools

import jax
import jax.numpy as jnp
from jax import lax
from jax.experimental import pallas as pl
from jax.experimental.pallas import tpu as pltpu
from jax.sharding import PartitionSpec as P

CAP = 3
RB_DEV = 32


gram_shift = 0.001

MIB = 2**20
IMAGE_STEP = 2048
PART_STEP = 768
LATE = 2
PACK_SPARE = 8
BASIS_SLOTS = 2 * CAP
SMEM = pl.BlockSpec(memory_space=pltpu.SMEM)
VMEM = pl.BlockSpec(memory_space=pltpu.VMEM)
ANY = pl.BlockSpec(memory_space=pl.ANY)


def in_vmem(shape, dtype):
    return pltpu.VMEM(shape, dtype)


def held(value):
    return pltpu.with_memory_space_constraint(value, pltpu.VMEM)


def in_hbm(value):
    return pltpu.with_memory_space_constraint(value, pltpu.HBM)


def plan_kernel(block_count, me_ref, touched_ref, home_ref, request_ref, place_ref, used_ref):
    group_size = request_ref.shape[0]

    @pl.loop(0, group_size)
    def _(holder):
        used_ref[holder] = 0
        for slot in range(CAP):
            request_ref[holder, slot] = -1

    @pl.loop(0, touched_ref.shape[0])
    def _(entry):
        stored = home_ref[touched_ref[entry]]
        holder = lax.rem(lax.div(stored, block_count), group_size)
        slot = used_ref[holder]
        used_ref[holder] = slot + 1
        request_ref[holder, slot] = lax.rem(stored, block_count)
        place_ref[entry] = jnp.bitwise_xor(holder, me_ref[0]) * CAP + slot


def serve_kernel(me_ref, asked_ref, sketch_ref, *refs):
    served_refs, sem = refs[:-1], refs[-1]

    for differs, served_ref in enumerate(served_refs):
        for slot in range(CAP):
            row = jnp.maximum(asked_ref[jnp.bitwise_xor(me_ref[0], differs), slot], 0)
            pltpu.make_async_copy(sketch_ref.at[row], served_ref.at[slot], sem).start()

    for served_ref in served_refs:
        pltpu.make_async_copy(served_ref, served_ref, sem).wait()


FIELD = 6
BUNCH = 4


def pack(tile, ray, slot):
    return lax.shift_left(lax.shift_left(tile, FIELD) + ray, FIELD) + slot


def unpack(entry):
    mask = 2**FIELD - 1
    cell = lax.shift_right_logical(entry, FIELD)
    return lax.shift_right_logical(cell, FIELD), jnp.bitwise_and(cell, mask), jnp.bitwise_and(entry, mask)


def list_kernel(chunks, slots, ray_ref, col_ref, place_ref, list_ref, count_ref):
    room = list_ref.shape[0] // (2 * chunks)
    rays, half = RB_DEV // chunks, slots // 2

    @pl.loop(0, 2 * chunks)
    def _(which):
        count_ref[which] = 0

    @pl.loop(0, ray_ref.shape[0], unroll=4)
    def _(tile):
        ray, slot = ray_ref[tile], place_ref[col_ref[tile]]
        far = (slot >= half).astype(jnp.int32)
        which = far * chunks + lax.div(ray, rays)
        count = count_ref[which]
        list_ref[which * room + count] = pack(tile, ray, slot - far * half)
        count_ref[which] = count + 1

    @pl.loop(0, 2 * chunks)
    def _(which):
        for _ in range(BUNCH - 1):
            count = count_ref[which]

            @pl.when(jnp.bitwise_and(count, BUNCH - 1) != 0)
            def _(count=count):
                list_ref[which * room + count] = RB_DEV << FIELD
                count_ref[which] = count + 1


def fill(far, list_ref, count_ref, tiles_ref, dense_ref, sems):
    tile_size = tiles_ref.shape[1]
    rows, cols = dense_ref.shape[0] - tile_size, dense_ref.shape[1]
    chunks = rows // IMAGE_STEP
    room = list_ref.shape[0] // (2 * chunks)

    @pl.loop(0, rows // tile_size)
    def _(block):
        at = pl.multiple_of(block * tile_size, tile_size)
        dense_ref[pl.ds(at, tile_size), :] = jnp.zeros((tile_size, cols), dense_ref.dtype)

    for chunk in range(chunks):
        which = far * chunks + chunk

        @pl.loop(0, lax.shift_right_logical(count_ref[which], BUNCH.bit_length() - 1))
        def _(bunch, which=which, chunk=chunk):
            entries = [list_ref[which * room + bunch * BUNCH + i] for i in range(BUNCH)]
            for tile, ray, slot in map(unpack, entries):
                row = pl.multiple_of(ray * tile_size, tile_size)
                col = pl.multiple_of(slot * tile_size, tile_size)
                to = dense_ref.at[pl.ds(row, tile_size), pl.ds(col, tile_size)]
                pltpu.make_async_copy(tiles_ref.at[tile], to, sems.at[chunk]).start()


def filled(far, count_ref, tiles_ref, sems, chunk):
    count = count_ref[far * sems.shape[0] + chunk]
    size = 1
    while size <= tiles_ref.shape[0]:

        @pl.when(jnp.bitwise_and(count, size) != 0)
        def _(size=size):
            some = tiles_ref.at[:size]
            pltpu.make_async_copy(some, some, sems.at[chunk]).wait()

        size *= 2


def stack(refs, stacked_ref, sem):
    copies, at = [], 0
    for ref in refs:
        for i in range(ref.shape[0]):
            to = stacked_ref.at[at : at + ref.shape[1]]
            copies.append(pltpu.make_async_copy(ref.at[i], to, sem))
            at += ref.shape[1]
    for copy in copies:
        copy.start()


def load_kernel(ray_ref, col_ref, place_ref, tiles_ref, _, dense_ref, sem):
    count, tile_size, _ = tiles_ref.shape
    rows, cols = dense_ref.shape

    @pl.loop(0, rows // tile_size)
    def _(block):
        at = pl.multiple_of(block * tile_size, tile_size)
        dense_ref[pl.ds(at, tile_size), :] = jnp.zeros((tile_size, cols), dense_ref.dtype)

    @pl.loop(0, count, unroll=8)
    def _(tile):
        row = pl.multiple_of(ray_ref[tile] * tile_size, tile_size)
        col = pl.multiple_of(place_ref[col_ref[tile]] * tile_size, tile_size)
        to = dense_ref.at[pl.ds(row, tile_size), pl.ds(col, tile_size)]
        pltpu.make_async_copy(tiles_ref.at[tile], to, sem).start()

    pltpu.make_async_copy(tiles_ref, tiles_ref, sem).wait()


def half_of(far, kept, refs):
    if kept:
        dense_ref, *refs = refs
        cols = dense_ref.shape[1] // 2
        return dense_ref.at[:, far * cols : (far + 1) * cols], lambda chunk: None, refs
    list_ref, count_ref, tiles_ref, *refs = refs
    *refs, dense_ref, sems = refs
    fill(far, list_ref, count_ref, tiles_ref, dense_ref, sems)
    return dense_ref, functools.partial(filled, far, count_ref, tiles_ref, sems), refs


def near_kernel(kept, *refs):
    dense_ref, ready, refs = half_of(0, kept, refs)
    *sketch_refs, sum_ref, sketch_ref, sem = refs
    stack(sketch_refs, sketch_ref, sem)
    pltpu.make_async_copy(sketch_ref, sketch_ref, sem).wait()

    @pl.loop(0, sum_ref.shape[0] // IMAGE_STEP)
    def _(chunk):
        ready(chunk)
        rows = pl.ds(pl.multiple_of(chunk * IMAGE_STEP, IMAGE_STEP), IMAGE_STEP)
        sum_ref[rows, :] = jnp.dot(dense_ref[rows, :], sketch_ref[...], preferred_element_type=jnp.float32)


def hand_out(total, part_refs):
    tall = part_refs[0].shape[0]
    for i, part_ref in enumerate(part_refs):
        part_ref[...] = total[:, i * tall : (i + 1) * tall].T.astype(part_ref.dtype)


def parts(images_ref, dense_ref, part_refs):
    rows, tall = images_ref.shape[1], part_refs[0].shape[0]
    each = PART_STEP // tall
    for first in range(0, len(part_refs), each):
        cols = dense_ref[:rows, first * tall : (first + each) * tall]
        part = jnp.dot(images_ref[...], cols, preferred_element_type=jnp.float32)
        hand_out(part, part_refs[first : first + each])


def far_kernel(holders, late, kept, *refs):
    dense_ref, ready, refs = half_of(1, kept, refs)
    sum_ref, *refs = refs
    sketch_refs, (token_ref, images_ref) = refs[:holders], refs[holders : holders + 2]
    *part_refs, sketch_ref, sem = refs[holders + 2 :]
    token_ref[...] = jnp.zeros(token_ref.shape, token_ref.dtype)
    stack(sketch_refs, sketch_ref, sem)
    pltpu.make_async_copy(sketch_ref, sketch_ref, sem).wait()

    @pl.loop(0, sum_ref.shape[0] // IMAGE_STEP)
    def _(chunk):
        ready(chunk)
        rows = pl.ds(pl.multiple_of(chunk * IMAGE_STEP, IMAGE_STEP), IMAGE_STEP)
        image = sum_ref[rows, :] + jnp.dot(dense_ref[rows, :], sketch_ref[...], preferred_element_type=jnp.float32)
        images_ref[:, rows] = image.astype(jnp.bfloat16).T

    parts(images_ref, dense_ref, part_refs)


def rest_kernel(late, kept, *refs):
    all_ref = refs[0]
    dense_ref, ready, refs = half_of(0, kept, refs)
    images_ref, _, *part_refs = refs

    @pl.loop(0, images_ref.shape[1] // IMAGE_STEP)
    def _(chunk):
        ready(chunk)

    parts(images_ref, dense_ref, part_refs[: len(part_refs) - late])
    if late:
        first = all_ref.shape[1] - late * part_refs[0].shape[0]
        parts(images_ref, all_ref.at[:, first:], part_refs[len(part_refs) - late :])


def zero_kernel(out_ref, zeros_ref, sem):
    rows = zeros_ref.shape[0]
    zeros_ref[...] = jnp.zeros(zeros_ref.shape, zeros_ref.dtype)

    @pl.loop(0, out_ref.shape[0] // rows)
    def _(chunk):
        pltpu.make_async_copy(zeros_ref, out_ref.at[pl.ds(chunk * rows, rows)], sem).start()

    pltpu.make_async_copy(out_ref, out_ref, sem).wait()


def split(value):
    high = value.astype(jnp.bfloat16)
    return high, (value - high.astype(jnp.float32)).astype(jnp.bfloat16)


def gather_kernel(me_ref, asked_ref, *refs):
    arrived_refs, (split_ref, pack_ref, block_ref, normal_ref, gram_ref, seen_ref) = refs[:-6], refs[-6:]
    slots, tile_size, width = normal_ref.shape

    @pl.loop(0, seen_ref.shape[0])
    def _(row):
        seen_ref[row] = -1

    @pl.loop(0, slots)
    def _(slot):
        block_ref[slot] = -1

    normal_ref[...] = jnp.zeros(normal_ref.shape, normal_ref.dtype)
    filled = 0
    for differs, arrived_ref in enumerate(arrived_refs):
        for slot in range(CAP):
            row = asked_ref[jnp.bitwise_xor(me_ref[0], differs), slot]
            safe = jnp.maximum(row, 0)
            known = seen_ref[safe]
            fresh = jnp.logical_and(row >= 0, known < 0)
            at = jnp.where(known < 0, filled, known)

            @pl.when(row >= 0)
            def _(at=at, safe=safe, arrived_ref=arrived_ref, slot=slot):
                seen_ref[safe] = at
                block_ref[at] = safe
                normal_ref[at] += arrived_ref[pl.ds(slot * tile_size, tile_size), :].astype(jnp.float32)

            filled = jnp.where(fresh, filled + 1, filled)

    gram_ref[...] = jnp.zeros(gram_ref.shape, gram_ref.dtype)
    tall = BASIS_SLOTS * tile_size

    @pl.loop(0, slots // BASIS_SLOTS)
    def _(chunk):
        at = pl.multiple_of(chunk * tall, tall)
        rows = jnp.concatenate([normal_ref[chunk * BASIS_SLOTS + i] for i in range(BASIS_SLOTS)], axis=0)
        high, low = split(rows)
        both_rows = jnp.concatenate([high, low], axis=1)
        split_ref[pl.ds(at, tall), :] = both_rows
        both = lax.dot_general(high, both_rows, (((0,), (0,)), ((), ())), preferred_element_type=jnp.float32)
        cross = both[:, width:]
        gram_ref[...] += both[:, :width] + cross + cross.T

    pack_ref[...] = packed(gram_ref[...])


def packed(gram):
    half = gram.shape[0] // 2
    top, bottom = gram[:half], pltpu.roll(gram[half:], half, 1)
    row = lax.broadcasted_iota(jnp.int32, top.shape, 0)
    col = lax.broadcasted_iota(jnp.int32, top.shape, 1)
    diagonal = jnp.sum(jnp.where(col == row, bottom, 0.0), axis=0, keepdims=True)
    last = jnp.broadcast_to(diagonal, (PACK_SPARE, gram.shape[1]))
    return jnp.concatenate([jnp.where(col >= row, top, bottom), last], axis=0)


def unpacked(pack):
    half = pack.shape[0] - PACK_SPARE
    top, diagonal = pack[:half], pack[half : half + 1]
    row = lax.broadcasted_iota(jnp.int32, top.shape, 0)
    col = lax.broadcasted_iota(jnp.int32, top.shape, 1)
    low = jnp.where(col < row, top, jnp.where(col == row, diagonal, 0.0))
    turned = jnp.concatenate([low, jnp.zeros_like(low)], axis=0).T[:half]
    upper = jnp.concatenate([jnp.where(col >= row, top, 0.0), pltpu.roll(turned, half, 1)], axis=0)
    row = lax.broadcasted_iota(jnp.int32, upper.shape, 0)
    col = lax.broadcasted_iota(jnp.int32, upper.shape, 1)
    return upper + jnp.where(col > row, upper, 0.0).T


def spread(value, like):
    return jnp.broadcast_to(value, like.shape)


def factor(gram, inverse_ref):
    panel, width = gram[0].shape
    gram = list(gram)
    row_at = lax.broadcasted_iota(jnp.int32, (panel, width), 0)
    lane = lax.broadcasted_iota(jnp.int32, (panel, width), 1)
    right = [jnp.where(lane == row_at + panel * i, 1.0, 0.0) for i in range(len(gram))]
    upper = []
    for p in range(len(gram)):
        start = panel * p
        columns = [
            [spread(rows[:, start + k : start + k + 1], rows) for k in range(panel)] for rows in gram[p:]
        ]
        corner = list(columns[0])
        left_rows, right_rows = gram[p], right[p]
        upper_rows, inverse_rows = jnp.zeros_like(left_rows), jnp.zeros_like(left_rows)
        for k in range(panel):
            pivot = spread(corner[k][k : k + 1], left_rows)
            reciprocal, root = 1.0 / pivot, lax.rsqrt(pivot)
            here = row_at == k
            left_row, right_row = spread(left_rows[k : k + 1], left_rows), spread(right_rows[k : k + 1], left_rows)
            upper_rows = jnp.where(here, left_row * root, upper_rows)
            inverse_rows = jnp.where(here, right_row * root, inverse_rows)
            by = jnp.where(here, -1.0, corner[k])
            for j in range(k + 1, panel):
                scaled = spread(corner[j][k : k + 1], left_rows) * reciprocal
                corner[j] = jnp.where(here, 0.0, corner[j]) - by * scaled
            left_rows = jnp.where(here, 0.0, left_rows) - by * (left_row * reciprocal)
            right_rows = jnp.where(here, 0.0, right_rows) - by * (right_row * reciprocal)
        upper.append(jnp.where(lane >= row_at + start, upper_rows, 0.0))
        inverse_ref[pl.ds(start, panel), :] = jnp.where(lane <= row_at + start, inverse_rows, 0.0)
        left_each = [spread(left_rows[k : k + 1], left_rows) for k in range(panel)]
        right_each = [spread(right_rows[k : k + 1], left_rows) for k in range(panel)]
        for i in range(p + 1, len(gram)):
            by = columns[i - p]
            gram[i] = gram[i] - total([b * row for b, row in zip(by, left_each)])
            right[i] = right[i] - total([b * row for b, row in zip(by, right_each)])
    return upper


def total(terms):
    while len(terms) > 1:
        terms = [sum(terms[i + 1 : i + 2], terms[i]) for i in range(0, len(terms), 2)]
    return terms[0]


def finish_kernel(voxels, block_ref, pack_ref, normal_ref, zeroed_ref, basis_ref, factor_ref, work_ref, out_ref, sem):
    width = factor_ref.shape[0]
    slots, tile_size, _ = out_ref.shape
    panel = 8
    row_at = lax.broadcasted_iota(jnp.int32, (panel, width), 0)
    lane = lax.broadcasted_iota(jnp.int32, (panel, width), 1)
    whole = unpacked(pack_ref[...])
    gram = []
    for start in range(0, width, panel):
        shift = jnp.where(lane == row_at + start, gram_shift, 0.0)
        gram.append(whole[start : start + panel] / voxels + shift)
    for i, rows in enumerate(factor(gram, work_ref)):
        factor_ref[pl.ds(panel * i, panel), :] = rows
    inverse = work_ref[...].T
    high, low = split(inverse)
    twice = jnp.concatenate([high, high], axis=0)
    tall = BASIS_SLOTS * tile_size

    def copy(slot):
        at = pl.multiple_of(block_ref[slot] * tile_size, tile_size)
        return pltpu.make_async_copy(out_ref.at[slot], basis_ref.at[pl.ds(at, tile_size)], sem.at[slot])

    @pl.loop(0, slots // BASIS_SLOTS)
    def _(chunk):
        rows = pl.ds(pl.multiple_of(chunk * tall, tall), tall)
        both = normal_ref[rows, :]
        value = jnp.dot(both, twice, preferred_element_type=jnp.float32)
        value += jnp.dot(both[:, :width], low, preferred_element_type=jnp.float32)
        for i in range(BASIS_SLOTS):
            slot = chunk * BASIS_SLOTS + i
            out_ref[slot] = value[i * tile_size : (i + 1) * tile_size]

            @pl.when(block_ref[slot] >= 0)
            def _(slot=slot):
                copy(slot).start()

    @pl.loop(0, slots)
    def _(slot):
        @pl.when(block_ref[slot] >= 0)
        def _():
            copy(slot).wait()


def summed(value, axes):
    outer, inner = (lax.axis_size(axis) for axis in axes)

    def other(bits):
        return lax.ppermute(value, axes, [(i, i ^ bits) for i in range(outer * inner)])

    def powers(low, high):
        return [1 << i for i in range(low.bit_length() - 1, high.bit_length() - 1)]

    core, *rest = powers(inner, outer * inner)
    near = powers(1, inner)
    odd = len(near) % 2
    bits = near[:odd] + rest + near[odd:]
    value = value + other(core)
    for i in range(0, len(bits) - 1, 2):
        one, two = bits[i : i + 2]
        value = (value + other(one)) + (other(two) + other(one ^ two))
    if len(bits) % 2:
        value = value + other(bits[-1])
    return value


def exchanged(values, first):
    size = lax.axis_size("dev")
    return [
        lax.ppermute(value, "dev", [(j, j ^ (first + i)) for j in range(size)]) for i, value in enumerate(values)
    ]


def local(tiles, tile_ray, tile_col, touched, home, sketch):
    group_size = lax.axis_size("dev")
    tile_size = tiles.shape[1]
    width = sketch.shape[1]
    block_count = sketch.shape[0] // tile_size
    ntouch = touched.shape[0]
    slots = group_size * CAP
    voxels = sketch.shape[0] * lax.axis_size("grp") * group_size

    half = group_size // 2
    rows, tall = RB_DEV * tile_size, CAP * tile_size
    me = lax.axis_index("dev").astype(jnp.int32).reshape(1)

    request, place = pl.pallas_call(
        functools.partial(plan_kernel, block_count),
        out_shape=(
            jax.ShapeDtypeStruct((group_size, CAP), jnp.int32),
            jax.ShapeDtypeStruct((ntouch,), jnp.int32),
        ),
        in_specs=[SMEM, SMEM, SMEM],
        out_specs=(SMEM, SMEM),
        scratch_shapes=[pltpu.SMEM((group_size,), jnp.int32)],
        name="plan",
    )(me, touched, home)
    kept = rows * slots * tile_size * tiles.dtype.itemsize <= 24 * MIB
    chunks = rows // IMAGE_STEP
    if not kept:
        room = min(RB_DEV // chunks * slots // 2, tiles.shape[0] + BUNCH)
        listed, counts = pl.pallas_call(
            functools.partial(list_kernel, chunks, slots),
            out_shape=(
                jax.ShapeDtypeStruct((2 * chunks * room,), jnp.int32),
                jax.ShapeDtypeStruct((2 * chunks,), jnp.int32),
            ),
            in_specs=[SMEM, SMEM, SMEM],
            out_specs=(SMEM, SMEM),
            name="list",
        )(tile_ray, tile_col, place)
        tile_operands, tile_specs = [listed, counts, in_hbm(tiles)], [SMEM, SMEM, ANY]
        tile_scratch = [
            pltpu.VMEM((rows + tile_size, half * tall), tiles.dtype),
            pltpu.SemaphoreType.DMA((chunks,)),
        ]
    asked = held(lax.all_to_all(request, "dev", split_axis=0, concat_axis=0, tiled=True))
    served = pl.pallas_call(
        serve_kernel,
        out_shape=[in_vmem((CAP, tile_size, width), sketch.dtype)] * group_size,
        in_specs=[SMEM, SMEM, ANY],
        out_specs=[VMEM] * group_size,
        scratch_shapes=[pltpu.SemaphoreType.DMA],
        compiler_params=pltpu.CompilerParams(vmem_limit_bytes=8 * MIB),
        name="serve",
    )(me, asked, in_hbm(sketch.reshape(block_count, tile_size, width)))
    replies = [served[0]] + exchanged(served[1:], 1)

    if kept:
        dense = pl.pallas_call(
            load_kernel,
            out_shape=in_vmem((rows, slots * tile_size), tiles.dtype),
            in_specs=[SMEM, SMEM, SMEM, ANY, ANY],
            out_specs=VMEM,
            scratch_shapes=[pltpu.SemaphoreType.DMA],
            compiler_params=pltpu.CompilerParams(vmem_limit_bytes=8 * MIB),
            name="load",
        )(in_hbm(tile_ray), in_hbm(tile_col), in_hbm(place), in_hbm(tiles), served[0])
        tile_operands, tile_specs, tile_scratch = [held(dense)], [VMEM], []

    def with_tiles(kernel, outs, specs, operands, scratch, name, flops):
        return pl.pallas_call(
            functools.partial(kernel, kept),
            out_shape=outs,
            in_specs=tile_specs + specs,
            out_specs=[VMEM] * len(outs),
            scratch_shapes=scratch + tile_scratch,
            compiler_params=pltpu.CompilerParams(vmem_limit_bytes=(12 if kept else 40) * MIB),
            cost_estimate=pl.CostEstimate(flops=flops, bytes_accessed=tiles.size, transcendentals=0),
            name=name,
        )(*tile_operands, *operands)

    late = LATE if kept else 0
    flops = 2 * rows * half * tall * width
    stacked = [pltpu.VMEM((half * tall, width), sketch.dtype), pltpu.SemaphoreType.DMA]
    (begun,) = with_tiles(
        near_kernel,
        [jax.ShapeDtypeStruct((rows, width), jnp.float32)],
        [ANY] * half,
        replies[:half],
        stacked,
        "images_near",
        flops,
    )
    token, images, *far_parts = with_tiles(
        functools.partial(far_kernel, half, late),
        [
            jax.ShapeDtypeStruct((8, width), jnp.float32),
            jax.ShapeDtypeStruct((width, rows), jnp.bfloat16),
        ]
        + [jax.ShapeDtypeStruct((tall, width), jnp.bfloat16)] * (half - late),
        [VMEM] + [ANY] * half,
        [begun] + replies[half:],
        stacked,
        "images_far",
        2 * flops,
    )
    far_arrived = exchanged(far_parts, half)
    own_part, *near_parts = with_tiles(
        functools.partial(rest_kernel, late),
        [jax.ShapeDtypeStruct((tall, width), jnp.float32)]
        + [jax.ShapeDtypeStruct((tall, width), jnp.bfloat16)] * (half - 1 + late),
        [VMEM, ANY],
        [images, exchanged([token], 1)[0]],
        [],
        "parts_near",
        flops,
    )
    far_arrived += exchanged(near_parts[half - 1 :], group_size - late)
    arrived = [own_part] + exchanged(near_parts[: half - 1], 1) + far_arrived

    zeroed = pl.pallas_call(
        zero_kernel,
        out_shape=jax.ShapeDtypeStruct(sketch.shape, jnp.float32),
        in_specs=[],
        out_specs=ANY,
        scratch_shapes=[pltpu.VMEM((sketch.shape[0] // 8, width), jnp.float32), pltpu.SemaphoreType.DMA],
        name="zeros",
    )()
    normal, gram, blocks = pl.pallas_call(
        gather_kernel,
        out_shape=(
            in_vmem((slots * tile_size, 2 * width), jnp.bfloat16),
            jax.ShapeDtypeStruct((width // 2 + PACK_SPARE, width), jnp.float32),
            jax.ShapeDtypeStruct((slots,), jnp.int32),
        ),
        in_specs=[SMEM, SMEM] + [VMEM] * group_size,
        out_specs=(VMEM, VMEM, SMEM),
        scratch_shapes=[
            pltpu.VMEM((slots, tile_size, width), jnp.float32),
            pltpu.VMEM((width, width), jnp.float32),
            pltpu.SMEM((block_count,), jnp.int32),
        ],
        compiler_params=pltpu.CompilerParams(vmem_limit_bytes=16 * MIB),
        name="collect",
    )(me, asked, *arrived)
    gram = summed(gram, ("grp", "dev"))
    return pl.pallas_call(
        functools.partial(finish_kernel, voxels),
        out_shape=(
            jax.ShapeDtypeStruct(sketch.shape, jnp.float32),
            jax.ShapeDtypeStruct((width, width), jnp.float32),
        ),
        in_specs=[SMEM, VMEM, VMEM, ANY],
        out_specs=(ANY, VMEM),
        scratch_shapes=[
            pltpu.VMEM((width, width), jnp.float32),
            pltpu.VMEM((slots, tile_size, width), jnp.float32),
            pltpu.SemaphoreType.DMA((slots,)),
        ],
        input_output_aliases={3: 0},
        compiler_params=pltpu.CompilerParams(vmem_limit_bytes=16 * MIB),
        name="finish",
    )(blocks, gram, held(normal), zeroed)


def solution(mesh):
    in_specs = (
        P(("grp", "dev"), None, None),
        P(("grp", "dev")),
        P(("grp", "dev")),
        P(("grp", "dev")),
        P(),
        P(("grp", "dev"), None),
    )
    out_specs = (P(("grp", "dev"), None), P())
    return jax.shard_map(local, mesh=mesh, in_specs=in_specs, out_specs=out_specs, check_vma=False)
```
